32 devices in a mesh: cfg: 2 (over y), space: 8 (over z, x), tm: 2 (over core).
Axes of the slice: x: 2, y: 2, z: 4, core: 2. Of those that a mesh axis runs over, the one named last changes fastest.
Arguments:
- eigvecs: bfloat16 [4, 2, 3, 1536, 256], P(('cfg', 'tm'), None, None, 'space'), parts along dimension 0, may hold values from -6 to 6
- momenta: int32 [3, 3], replicated, may hold values from -2 to 2, as said below
- pair_list: int32 [8, 2], P('tm'), may hold values from 0 to 1
- panels: bfloat16 [16, 2, 1024, 1024], P(('cfg', 'tm'), None, 'space'), parts along dimension 0, may hold values from -6 to 6
Outputs:
- dressed: bfloat16 [16, 3, 2, 1024, 1024], P(('cfg', 'tm'), None, None, 'space'), parts along dimension 0
The draws below stay inside these ranges and needn't reach their ends.
There are 2 independent parts, one for each index of `cfg`. The reference program is written for one: setup_inputs(seed, part) draws one part's arguments, and reference() takes and returns one part's arrays. A program takes and returns all parts, laid end to end along the dimension named above; an argument that names none is the same for every part. Nothing has to cross between parts.
Inputs may be any that keep to these rules, and one draw needn't show every extreme that they name: `momenta`: the first component of every momentum is nonzero.
All inputs are finite; a program needn't handle non-finite values.
Results may differ from the reference program's by a relative error of at most 0.0075.
Values may be sent and summed in bfloat16 or wider, within the bound.
No kernel may reach another device: no remote copies, remote signals or barrier semaphores. Data moves between devices by JAX's collectives and lax.ppermute only.
A program may use at most 64 MiB of HBM per device.

```python
import math
import jax
import jax.numpy as jnp
from jax import lax

LX = 64
NEV = 256
NSPIN = 4
NCOL = 3
NMOM = 3
T_WIN = 2
SITES = 1536
NPAIR = 8


def draw_momenta(key, part):
    key_mag = jax.random.fold_in(key, 11)
    key_sign = jax.random.fold_in(key, 12)
    key_rest = jax.random.fold_in(key, 13)
    magnitude = jax.random.randint(key_mag, (NMOM, 1), 1, 3)
    sign_part = jax.random.randint(key_sign, (NMOM, 1), 0, 2) * 2 - 1
    others = jax.random.randint(key_rest, (NMOM, 2), -2, 3)
    return jnp.concatenate([magnitude * sign_part, others], 1).astype(jnp.int32)


def place_ends(entries, key, smallest, top_value):
    extent = entries.shape
    index_at = [jax.random.randint(jax.random.fold_in(key, axis), (), 0, extent[axis]) for axis in range(len(extent))]
    entries = entries.at[tuple(index_at)].set(smallest)
    longest = extent.index(max(extent))
    index_at[longest] = (index_at[longest] + 1) % extent[longest]
    return entries.at[tuple(index_at)].set(top_value)


def block_levels(rng, extent, cuts, least, top_value):
    loudness, own = 1.0, jax.random.fold_in(rng, 6)
    for dim, shards_of in cuts:
        steps = jnp.exp(jax.random.uniform(jax.random.fold_in(own, dim), (shards_of,), jnp.float32, least / len(cuts), top_value / len(cuts)))
        loudness = loudness * jnp.repeat(steps, extent[dim] // shards_of).reshape([-1 if axis == dim else 1 for axis in range(len(extent))])
    return loudness


def scatter_about(stream_key, extent, width, limit, pieces=(), kind=jnp.bfloat16):
    factor_of = block_levels(stream_key, extent, pieces, -0.22, 0.18) if pieces else 1.0
    drawn = jax.random.normal(stream_key, extent, jnp.float32) * width * factor_of
    return jnp.minimum(jnp.maximum(drawn, -limit), limit).astype(kind)


def setup_inputs(seed: int = 0, part: int = 0) -> dict:
    key_list = jax.random.split(jax.random.key(seed), 5)
    own_keys = jax.random.split(jax.random.fold_in(key_list[4], part), 5)
    return {
        "eigvecs": scatter_about(own_keys[0], (T_WIN, 2, NCOL, SITES, NEV), 1.0, 6.0, ((0, 2), (3, 8))),
        "momenta": draw_momenta(jax.random.fold_in(key_list[4], 71), part),
        "pair_list": place_ends(jax.random.randint(key_list[2], (NPAIR, 2), 0, T_WIN), jax.random.fold_in(key_list[2], 1), 0, T_WIN - 1).astype(jnp.int32),
        "panels": scatter_about(own_keys[3], (NPAIR, 2, NSPIN * NEV, NSPIN * NEV), 1.0, 6.0, ((0, 2), (2, 8))),
    }


def phase_table(momenta, site_index):
    xpos = site_index % LX
    ypos = site_index // LX % LX
    zpos = site_index // (LX * LX)
    wave = momenta[:, 0:1] * xpos[None, :] + momenta[:, 1:2] * ypos[None, :] + momenta[:, 2:3] * zpos[None, :]
    wave = jnp.mod(wave, LX)
    angle = wave.astype(jnp.float32) * jnp.float32(2.0 * math.pi / LX)
    return (jnp.cos(angle), jnp.sin(angle))

def phased_block(cosine, sine_part, real_part, imag_part):
    cos_col = cosine[:, None]
    sin_col = sine_part[:, None]
    wave_re = cos_col * real_part + sin_col * imag_part
    wave_im = cos_col * imag_part - sin_col * real_part
    upper = jnp.concatenate([wave_re, wave_im], -1)
    lower = jnp.concatenate([wave_im, -wave_re], -1)
    return jnp.stack([upper, lower], -4).astype(jnp.bfloat16)

def reference(eigvecs, momenta, pair_list, panels):
    site_index = jnp.arange(SITES, dtype=jnp.int32)
    cosine, sine_part = phase_table(momenta, site_index)
    factor = 1.0 / math.sqrt(6.0 * SITES * NEV)
    fields = []
    for slot in range(T_WIN):
        block = eigvecs[slot].astype(jnp.float32)
        per_moment = []
        for moment in range(NMOM):
            phased = phased_block(cosine[moment], sine_part[moment], block[0], block[1])
            gram_sum = jnp.einsum('rcsk,rcsl->kl', block, phased.astype(jnp.float32), precision=lax.Precision.HIGHEST)
            per_moment.append((factor * gram_sum).astype(jnp.bfloat16))
        fields.append(jnp.stack(per_moment, 0))
    meson_fields = jnp.stack(fields, 0)
    results = []
    for pair in range(NPAIR):
        source_fields = meson_fields[pair_list[pair, 0]].reshape(NMOM, NEV, 2, NEV).astype(jnp.float32)
        sink_fields = meson_fields[pair_list[pair, 1]].reshape(NMOM, NEV, 2, NEV).astype(jnp.float32)
        panel_parts = panels[pair].reshape(2, NSPIN * NEV, NSPIN, NEV).astype(jnp.float32)
        panel_re = panel_parts[0]
        panel_im = panel_parts[1]
        panel_mix = jnp.stack([jnp.stack([panel_re, panel_im], 0), jnp.stack([panel_im, -panel_re], 0)], 0)
        right_dressed = jnp.einsum('orxbk,mlrk->moxbl', panel_mix, source_fields, precision=lax.Precision.HIGHEST)
        right_dressed = right_dressed.astype(jnp.bfloat16).astype(jnp.float32)
        right_dressed = right_dressed.reshape(NMOM, 2, NSPIN, NEV, NSPIN * NEV)
        right_re = right_dressed[:, 0]
        right_im = right_dressed[:, 1]
        mixed_parts = jnp.stack([jnp.stack([right_re, -right_im], 1), jnp.stack([right_im, right_re], 1)], 1)
        dressed_pair = jnp.einsum('morajc,mkrj->mocak', mixed_parts, sink_fields, precision=lax.Precision.HIGHEST)
        results.append(dressed_pair.reshape(NMOM, 2, NSPIN * NEV, NSPIN * NEV).astype(jnp.bfloat16))
    return jnp.stack(results, 0)
```

```python
import functools
import math

import jax
import jax.numpy as jnp
from jax import lax
from jax.experimental import pallas as pl
from jax.experimental.pallas import tpu as pltpu
from jax.sharding import PartitionSpec as P

LX = 64
LX_BITS = LX.bit_length() - 1
F32, BF16 = jnp.float32, jnp.bfloat16
VMEM_LIMIT = 40 * 1024 * 1024


def params(steps=0):
    return pltpu.CompilerParams(
        vmem_limit_bytes=VMEM_LIMIT, dimension_semantics=("arbitrary",) * steps or None
    )


def cost(flops, bytes_accessed):
    return pl.CostEstimate(flops=int(flops), bytes_accessed=int(bytes_accessed), transcendentals=0)


def gram_kernel(factor, place, momenta, eig, send, keep, phased, total):
    colors, sites, vectors = eig.shape[1:]
    moms = send.shape[0]
    half = send.shape[1]
    site = place[0] * sites + lax.broadcasted_iota(jnp.int32, (sites, 128), 0)
    lane = lax.broadcasted_iota(jnp.int32, (sites, 128), 1)
    coords = (site & (LX - 1), (site >> LX_BITS) & (LX - 1), site >> (2 * LX_BITS))
    wave = jnp.zeros((sites, 128), jnp.int32)
    for m in range(moms):
        mine = sum(momenta[m, j] * coords[j] for j in range(3))
        wave = jnp.where(lane == m, mine, wave)
    angle = (wave & (LX - 1)).astype(F32) * F32(2.0 * math.pi / LX)
    cosine, sine = jnp.cos(angle), jnp.sin(angle)
    rows = colors * sites
    both = eig[...].reshape(2 * rows, vectors)
    bit = place[1]
    for m in range(moms):
        c, s = cosine[:, m : m + 1], sine[:, m : m + 1]
        for color in range(colors):
            re, im = eig[0, color].astype(F32), eig[1, color].astype(F32)
            wave_re, wave_im = c * re + s * im, c * im - s * re
            at = color * sites
            phased[at : at + sites, :vectors] = wave_re.astype(BF16)
            phased[at : at + sites, vectors:] = wave_im.astype(BF16)
            at += rows
            phased[at : at + sites, :vectors] = wave_im.astype(BF16)
            phased[at : at + sites, vectors:] = (-wave_re).astype(BF16)
        total[...] = factor * lax.dot_general(
            both, phased[...], (((0,), (0,)), ((), ())), preferred_element_type=F32
        )
        send[m] = total[pl.ds(pl.multiple_of((1 - bit) * half, half), half), :].astype(BF16)
        keep[m] = total[pl.ds(pl.multiple_of(bit * half, half), half), :]


def gram_halves(eig, momenta, place, factor):
    _, colors, sites, vectors = eig.shape
    moms = momenta.shape[0]
    shape = (moms, vectors // 2, 2 * vectors)
    smem = pl.BlockSpec(memory_space=pltpu.SMEM)
    vmem = pl.BlockSpec(memory_space=pltpu.VMEM)
    return pl.pallas_call(
        functools.partial(gram_kernel, factor),
        out_shape=(jax.ShapeDtypeStruct(shape, BF16), jax.ShapeDtypeStruct(shape, F32)),
        in_specs=[smem, smem, vmem],
        out_specs=(vmem, vmem),
        scratch_shapes=[
            pltpu.VMEM((2 * colors * sites, 2 * vectors), BF16),
            pltpu.VMEM((vectors, 2 * vectors), F32),
        ],
        compiler_params=params(),
        cost_estimate=cost(4 * colors * sites * vectors * moms * 2 * vectors, 3 * 2**20),
        name="gram",
    )(place, momenta, eig)


def fold_kernel(bit_at, place, keep_in, came, send, keep):
    half = send.shape[1]
    bit = place[bit_at]
    own = pl.ds(pl.multiple_of(bit * half, half), half)
    off = pl.ds(pl.multiple_of((1 - bit) * half, half), half)
    keep[...] = keep_in[:, own, :] + came[:, own, :].astype(F32)
    send[...] = (keep_in[:, off, :] + came[:, off, :].astype(F32)).astype(BF16)


def fold(keep, came, place, bit_at):
    moms, rows, width = keep.shape
    shape = (moms, rows // 2, width)
    smem = pl.BlockSpec(memory_space=pltpu.SMEM)
    vmem = pl.BlockSpec(memory_space=pltpu.VMEM)
    return pl.pallas_call(
        functools.partial(fold_kernel, bit_at),
        out_shape=(jax.ShapeDtypeStruct(shape, BF16), jax.ShapeDtypeStruct(shape, F32)),
        in_specs=[smem, vmem, vmem],
        out_specs=(vmem, vmem),
        compiler_params=params(),
        cost_estimate=cost(keep.size, 8 * keep.size),
        name="fold",
    )(place, keep, came)


def dress_kernel(count, chained, place, other_src, other_snk, own, oth, *refs):
    mine, near = refs[:count], refs[count : 2 * count]
    out = refs[2 * count + chained]
    left, sink, panel = refs[2 * count + chained + 1 :]
    pieces, moms, piece_rows, width = own.shape
    vectors = width // 2
    columns = out.shape[3]
    pair, step = pl.program_id(0), pl.program_id(1)
    here, x = place[4], place[2]
    block = mine[0].shape[2]

    def load(field):
        def source():
            for m in range(moms):
                for i in range(columns // piece_rows):
                    q = x * (columns // piece_rows) + i
                    rows = field[q ^ here, m]
                    re, im = rows[:, :vectors], rows[:, vectors:]
                    at = 2 * m * columns + i * piece_rows
                    left[at : at + piece_rows, :vectors] = re
                    left[at : at + piece_rows, vectors:] = im
                    at += columns
                    left[at : at + piece_rows, :vectors] = -im
                    left[at : at + piece_rows, vectors:] = re

        def drain():
            for m in range(moms):
                for q in range(pieces):
                    rows = field[here ^ q, m]
                    sink[m, 0, q * piece_rows : (q + 1) * piece_rows] = rows[:, :vectors]
                    sink[m, 1, q * piece_rows : (q + 1) * piece_rows] = rows[:, vectors:]

        return source, drain

    own_source, own_drain = load(own)
    oth_source, oth_drain = load(oth)
    first = step == 0
    src, snk = other_src[pair], other_snk[pair]
    pl.when(first & (src == 0))(own_source)
    pl.when(first & (src != 0))(oth_source)
    pl.when(first & (snk == 0))(own_drain)
    pl.when(first & (snk != 0))(oth_drain)

    at_mine = pl.ds(pl.multiple_of(x * block, block), block)
    at_near = pl.ds(pl.multiple_of((1 - x) * block, block), block)
    for k in range(count):

        @pl.when(step == k)
        def _(k=k):
            for part in range(2):
                lanes = slice(part * vectors, (part + 1) * vectors)
                panel[at_mine, lanes] = mine[k][0, part]
                panel[at_near, lanes] = near[k][0, part]

    contract = (((1,), (1,)), ((), ()))
    right = lax.dot_general(left[...], panel[...], contract, preferred_element_type=F32).astype(BF16)
    for m in range(moms):
        rows = right[2 * m * columns : 2 * (m + 1) * columns]
        with_re = lax.dot_general(rows, sink[m, 0], contract, preferred_element_type=F32)
        with_im = lax.dot_general(rows, sink[m, 1], contract, preferred_element_type=F32)
        out[0, m, 0] = (with_re[:columns] - with_im[columns:]).astype(BF16)
        out[0, m, 1] = (with_im[:columns] + with_re[columns:]).astype(BF16)


def dress(out, out_shape, first_pair, dists, mine, near, own, oth, place, other_src, other_snk):
    pairs, _, block, vectors = mine[0].shape
    count = len(dists)
    moms = own.shape[1]
    columns = out_shape.shape[3]
    whole = pl.BlockSpec(memory_space=pltpu.VMEM)
    chunk = pl.BlockSpec((1, 2, block, vectors), lambda p, d, *_: (p, 0, 0, 0))

    def target(p, d, place, *_):
        dist = jnp.int32(dists[0])
        for k in range(1, count):
            dist = jnp.where(d == k, dists[k], dist)
        return (p + first_pair, 0, 0, 0, place[3] ^ dist)

    chained = out is not None
    operands = [own, oth, *mine, *near] + ([out] if chained else [])
    in_specs = [whole, whole] + [chunk] * (2 * count) + [pl.BlockSpec(memory_space=pl.ANY)] * chained
    macs = pairs * count * 2 * (2 * moms * columns) * (2 * vectors) * vectors
    return pl.pallas_call(
        functools.partial(dress_kernel, count, chained),
        out_shape=out_shape,
        grid_spec=pltpu.PrefetchScalarGridSpec(
            num_scalar_prefetch=3,
            grid=(pairs, count),
            in_specs=in_specs,
            out_specs=pl.BlockSpec((1, moms, 2, columns, vectors), target),
            scratch_shapes=[
                pltpu.VMEM((2 * moms * columns, 2 * vectors), BF16),
                pltpu.VMEM((moms, 2, vectors, vectors), BF16),
                pltpu.VMEM((2 * block, 2 * vectors), BF16),
            ],
        ),
        input_output_aliases={3 + len(operands) - 1: 0} if chained else {},
        compiler_params=params(2),
        cost_estimate=cost(2 * macs, 2**21),
        name="dress",
    )(place, other_src[first_pair : first_pair + pairs], other_snk[first_pair : first_pair + pairs], *operands)


def exchange(value, axis, mask):
    return lax.ppermute(value, axis, [(i, i ^ mask) for i in range(lax.axis_size(axis))])


def fast(eigvecs, momenta, pair_list, panels):
    vectors = eigvecs.shape[4]
    pair_count, _, rows, width = panels.shape
    moms = momenta.shape[0]
    space_count = lax.axis_size("space")
    spins = width // vectors
    space = lax.axis_index("space")
    tm = lax.axis_index("tm")
    x, z = space & 1, space >> 1
    masks = [1 << b for b in range(1, spins.bit_length())][:1] + [1] + [
        1 << b for b in range(2, spins.bit_length())
    ]
    bits = [(space & mask) // mask for mask in masks]
    here = sum(bit << (len(bits) - 1 - i) for i, bit in enumerate(bits))
    place = jnp.stack([space, bits[0], x, z, here] + bits[1:]).astype(jnp.int32)
    other = (pair_list != tm).astype(jnp.int32)
    other_src, other_snk = other[:, 0], other[:, 1]

    factor = 1.0 / math.sqrt(6.0 * eigvecs.shape[3] * space_count * vectors)
    send, keep = gram_halves(eigvecs[0], momenta, place, factor)
    for step, mask in enumerate(masks):
        came = exchange(send, "space", mask)
        if step + 1 < len(masks):
            send, keep = fold(keep, came, place, 5 + step)
    field = (keep + came.astype(F32)).astype(BF16)[None]
    for mask in masks[::-1]:
        field = jnp.concatenate([field, exchange(field, "space", mask)], 0)
    oth = exchange(field, "tm", 1)

    chunks = 2
    per = pair_count // chunks
    blocks = [
        lax.dynamic_slice_in_dim(panels, (z ^ d) * vectors, vectors, axis=3) for d in range(spins)
    ]
    mine = {(0, c): blocks[0][c * per : (c + 1) * per] for c in range(chunks)}
    order = (3, 2, 1)
    for c in range(chunks):
        for d in order:
            mine[d, c] = exchange(blocks[d][c * per : (c + 1) * per], "space", d << 1)
    near = {}
    for c in range(chunks):
        for d in (0, *order):
            near[d, c] = exchange(mine[d, c], "space", 1)
    columns = width // space_count
    out_shape = jax.ShapeDtypeStruct((pair_count, moms, 2, columns, width), BF16)
    out = None
    for c in range(chunks):
        out = dress(
            out, out_shape, c * per, list(range(spins)),
            [mine[d, c] for d in range(spins)], [near[d, c] for d in range(spins)],
            field, oth, place, other_src, other_snk,
        )
    return out


def phased_block(cosine, sine_part, real_part, imag_part):
    cos_col = cosine[:, None]
    sin_col = sine_part[:, None]
    wave_re = cos_col * real_part + sin_col * imag_part
    wave_im = cos_col * imag_part - sin_col * real_part
    upper = jnp.concatenate([wave_re, wave_im], -1)
    lower = jnp.concatenate([wave_im, -wave_re], -1)
    return jnp.stack([upper, lower], -4).astype(jnp.bfloat16)


def general(eigvecs, momenta, pair_list, panels):
    slice_count, _, colors, slab_sites, vectors = eigvecs.shape
    mom_count = momenta.shape[0]
    space_count = lax.axis_size("space")
    first_site = lax.axis_index("space") * slab_sites
    site_index = first_site + jnp.arange(slab_sites, dtype=jnp.int32)
    xpos = site_index % LX
    ypos = site_index // LX % LX
    zpos = site_index // (LX * LX)
    wave = (
        momenta[:, 0:1] * xpos[None, :]
        + momenta[:, 1:2] * ypos[None, :]
        + momenta[:, 2:3] * zpos[None, :]
    )
    wave = jnp.mod(wave, LX)
    angle = wave.astype(jnp.float32) * jnp.float32(2.0 * math.pi / LX)
    cosine = jnp.cos(angle)
    sine_part = jnp.sin(angle)
    factor = 1.0 / math.sqrt(6.0 * slab_sites * space_count * vectors)
    real_part = eigvecs[:, 0].astype(jnp.float32)
    imag_part = eigvecs[:, 1].astype(jnp.float32)
    phased_all = jnp.concatenate(
        [
            phased_block(cosine[moment], sine_part[moment], real_part, imag_part)
            for moment in range(mom_count)
        ],
        -1,
    )
    phased_all = phased_all.reshape(slice_count, 2, colors, slab_sites, mom_count, 2 * vectors)
    gram_local = jnp.einsum(
        "trcsk,trcsml->tmkl", eigvecs, phased_all, preferred_element_type=jnp.float32
    )
    gram_local = factor * gram_local
    summed = lax.psum(gram_local, "space")
    own_fields = summed.astype(jnp.bfloat16)
    meson_fields = lax.all_gather(own_fields, "tm", axis=0, tiled=True)
    pair_count = pair_list.shape[0]
    panel_rows = panels.shape[2]
    panel_width = panels.shape[3]
    spins = panel_width // vectors
    source_fields = jnp.take(meson_fields, pair_list[:, 0], axis=0).reshape(
        pair_count, mom_count, vectors, 2, vectors
    )
    sink_fields = jnp.take(meson_fields, pair_list[:, 1], axis=0).reshape(
        pair_count, mom_count, vectors, 2, vectors
    )
    panel_parts = panels.reshape(pair_count, 2, panel_rows, spins, vectors)
    panel_re = panel_parts[:, 0]
    panel_im = panel_parts[:, 1]
    panel_mix = jnp.stack(
        [jnp.stack([panel_re, panel_im], 1), jnp.stack([panel_im, -panel_re], 1)], 1
    )
    right_dressed = jnp.einsum(
        "porxbk,pmlrk->pmoxbl", panel_mix, source_fields, preferred_element_type=jnp.float32
    )
    right_dressed = right_dressed.astype(jnp.bfloat16).reshape(
        pair_count * mom_count, 2, panel_rows, panel_width
    )
    turned = lax.all_to_all(right_dressed, "space", split_axis=3, concat_axis=2, tiled=True)
    column_count = turned.shape[3]
    turned = turned.reshape(pair_count, mom_count, 2, spins, vectors, column_count)
    turned_re = turned[:, :, 0]
    turned_im = turned[:, :, 1]
    mixed_parts = jnp.stack(
        [jnp.stack([turned_re, -turned_im], 2), jnp.stack([turned_im, turned_re], 2)], 2
    )
    dressed = jnp.einsum(
        "pmorajc,pmkrj->pmocak", mixed_parts, sink_fields, preferred_element_type=jnp.float32
    )
    return dressed.reshape(pair_count, mom_count, 2, column_count, panel_width).astype(jnp.bfloat16)


def local(eigvecs, momenta, pair_list, panels):
    slices, _, _, sites, vectors = eigvecs.shape
    pairs, _, rows, width = panels.shape
    space_count = lax.axis_size("space")
    spins = width // vectors
    fits = (
        slices == 1
        and lax.axis_size("tm") == 2
        and space_count == 2 * spins
        and spins == 4
        and rows * space_count == width
        and rows % 128 == 0
        and (vectors // space_count) % 16 == 0
        and sites % 16 == 0
        and pairs % 2 == 0
        and momenta.shape[0] <= 8
    )
    return (fast if fits else general)(eigvecs, momenta, pair_list, panels)


def solution(mesh):
    placed = (
        P(("cfg", "tm"), None, None, "space", None),
        P(),
        P("tm", None),
        P(("cfg", "tm"), None, "space", None),
    )
    return jax.shard_map(
        local,
        mesh=mesh,
        in_specs=placed,
        out_specs=P(("cfg", "tm"), None, None, "space", None),
        check_vma=False,
    )
```

```python
import functools
import math

import jax
import jax.numpy as jnp
from jax import lax
from jax.experimental import pallas as pl
from jax.experimental.pallas import tpu as pltpu
from jax.sharding import PartitionSpec as P

LX = 64
LX_BITS = LX.bit_length() - 1
F32, BF16 = jnp.float32, jnp.bfloat16
SPACE, X, Z, Z_LOW, Z_HIGH, HERE_A, HERE_B = range(7)
VMEM_LIMIT = 24 * 1024 * 1024
CUT_VMEM = 24 * 1024 * 1024


def params(steps=0):
    return pltpu.CompilerParams(
        vmem_limit_bytes=VMEM_LIMIT, dimension_semantics=("arbitrary",) * steps or None
    )


def cost(flops, bytes_accessed):
    return pl.CostEstimate(flops=int(flops), bytes_accessed=int(bytes_accessed), transcendentals=0)


def gram_kernel(factor, place, momenta, eig, send_a, send_b, keep_a, keep_b, phased, total):
    colors, sites, vectors = eig.shape[1:]
    moms, half = send_a.shape[:2]
    site = place[SPACE] * sites + lax.broadcasted_iota(jnp.int32, (sites, 128), 0)
    lane = lax.broadcasted_iota(jnp.int32, (sites, 128), 1)
    coords = (site & (LX - 1), (site >> LX_BITS) & (LX - 1), site >> (2 * LX_BITS))
    wave = jnp.zeros((sites, 128), jnp.int32)
    for m in range(moms):
        mine = sum(momenta[m, j] * coords[j] for j in range(3))
        wave = jnp.where(lane == m, mine, wave)
    angle = (wave & (LX - 1)).astype(F32) * F32(2.0 * math.pi / LX)
    cosine, sine = jnp.cos(angle), jnp.sin(angle)
    rows = colors * sites
    both = eig[...].reshape(2 * rows, vectors)
    for m in range(moms):
        c, s = cosine[:, m : m + 1], sine[:, m : m + 1]
        for color in range(colors):
            re, im = eig[0, color].astype(F32), eig[1, color].astype(F32)
            wave_re, wave_im = c * re + s * im, c * im - s * re
            at = color * sites
            phased[at : at + sites, :vectors] = wave_re.astype(BF16)
            phased[at : at + sites, vectors:] = wave_im.astype(BF16)
            at += rows
            phased[at : at + sites, :vectors] = wave_im.astype(BF16)
            phased[at : at + sites, vectors:] = (-wave_re).astype(BF16)
        total[...] = factor * lax.dot_general(
            both, phased[...], (((0,), (0,)), ((), ())), preferred_element_type=F32
        )
        for send, keep, bit, lanes in (
            (send_a, keep_a, place[X], slice(None, vectors)),
            (send_b, keep_b, place[Z_LOW], slice(vectors, None)),
        ):
            send[m] = total[pl.ds(pl.multiple_of((1 - bit) * half, half), half), lanes].astype(BF16)
            keep[m] = total[pl.ds(pl.multiple_of(bit * half, half), half), lanes]


def gram_halves(eig, momenta, place, factor):
    _, colors, sites, vectors = eig.shape
    moms = momenta.shape[0]
    shape = (moms, vectors // 2, vectors)
    smem = pl.BlockSpec(memory_space=pltpu.SMEM)
    vmem = pl.BlockSpec(memory_space=pltpu.VMEM)
    return pl.pallas_call(
        functools.partial(gram_kernel, factor),
        out_shape=[jax.ShapeDtypeStruct(shape, kind) for kind in (BF16, BF16, F32, F32)],
        in_specs=[smem, smem, vmem],
        out_specs=[vmem] * 4,
        scratch_shapes=[
            pltpu.VMEM((2 * colors * sites, 2 * vectors), BF16),
            pltpu.VMEM((vectors, 2 * vectors), F32),
        ],
        compiler_params=params(),
        cost_estimate=cost(4 * colors * sites * vectors * moms * 2 * vectors, 3 * 2**20),
        name="gram",
    )(place, momenta, eig)


def cut_kernel(plan, place, panels, *refs):
    cuts, sems = refs[:-1], refs[-1]
    vectors = cuts[0].shape[3]
    copies = []
    for i, (d, first, _) in enumerate(plan):
        lanes = pl.ds(pl.multiple_of((place[Z] ^ d) * vectors, vectors), vectors)
        source = panels.at[first : first + cuts[i].shape[0], :, :, lanes]
        copies.append(pltpu.make_async_copy(source, cuts[i], sems.at[i]))
        copies[-1].start()
    for copy in copies:
        copy.wait()


def cut_panels(panels, vectors, plan, vmem, place):
    cuts = pl.pallas_call(
        functools.partial(cut_kernel, plan),
        out_shape=[jax.ShapeDtypeStruct((size, *panels.shape[1:3], vectors), BF16) for _, _, size in plan],
        in_specs=[pl.BlockSpec(memory_space=pltpu.SMEM), pl.BlockSpec(memory_space=pl.ANY)],
        out_specs=[pl.BlockSpec(memory_space=pltpu.VMEM)] * len(plan),
        scratch_shapes=[pltpu.SemaphoreType.DMA((len(plan),))],
        compiler_params=pltpu.CompilerParams(vmem_limit_bytes=vmem),
        cost_estimate=cost(0, 4 * panels.size),
        name="cut",
    )(place, panels)
    return {(d, first // size): cut for (d, first, size), cut in zip(plan, cuts)}


def fold_kernel(place, keep_a, keep_b, came_a, came_b, send_a, send_b, left_a, left_b):
    half = send_a.shape[1]
    for keep, came, bit, send, left in (
        (keep_a, came_a, place[Z_LOW], send_a, left_a),
        (keep_b, came_b, place[X], send_b, left_b),
    ):
        own = pl.ds(pl.multiple_of(bit * half, half), half)
        off = pl.ds(pl.multiple_of((1 - bit) * half, half), half)
        left[...] = keep[:, own, :] + came[:, own, :].astype(F32)
        send[...] = (keep[:, off, :] + came[:, off, :].astype(F32)).astype(BF16)


def join_kernel(place, keep_a, keep_b, came_a, came_b, send, left):
    half, width = send.shape[1:]
    bit = place[Z_HIGH]
    own = pl.ds(pl.multiple_of(bit * half, half), half)
    off = pl.ds(pl.multiple_of((1 - bit) * half, half), half)
    for keep, came, lanes in (
        (keep_a, came_a, slice(None, width // 2)),
        (keep_b, came_b, slice(width // 2, None)),
    ):
        left[:, :, lanes] = keep[:, own, :] + came[:, own, :].astype(F32)
        send[:, :, lanes] = (keep[:, off, :] + came[:, off, :].astype(F32)).astype(BF16)


def fold(kernel, keep_a, keep_b, came_a, came_b, place):
    moms, rows, width = keep_a.shape
    if kernel is join_kernel:
        shape, kinds = (moms, rows // 2, 2 * width), (BF16, F32)
    else:
        shape, kinds = (moms, rows // 2, width), (BF16, BF16, F32, F32)
    vmem = pl.BlockSpec(memory_space=pltpu.VMEM)
    return pl.pallas_call(
        kernel,
        out_shape=[jax.ShapeDtypeStruct(shape, kind) for kind in kinds],
        in_specs=[pl.BlockSpec(memory_space=pltpu.SMEM)] + [vmem] * 4,
        out_specs=[vmem] * len(kinds),
        compiler_params=params(),
        cost_estimate=cost(2 * keep_a.size, 16 * keep_a.size),
        name="fold",
    )(place, keep_a, keep_b, came_a, came_b)


def prepare_kernel(place, own_a, own_b, oth_a, oth_b, left, sink):
    pieces, moms, piece_rows, vectors = own_a.shape
    columns = left.shape[1] // (2 * moms)
    here_a, here_b, x = place[HERE_A], place[HERE_B], place[X]
    for t, (part_a, part_b) in enumerate(((own_a, own_b), (oth_a, oth_b))):
        for m in range(moms):
            for i in range(columns // piece_rows):
                q = x * (columns // piece_rows) + i
                re, im = part_a[q ^ here_a, m], part_b[q ^ here_b, m]
                at = 2 * m * columns + i * piece_rows
                left[t, at : at + piece_rows, :vectors] = re
                left[t, at : at + piece_rows, vectors:] = im
                at += columns
                left[t, at : at + piece_rows, :vectors] = -im
                left[t, at : at + piece_rows, vectors:] = re
            for q in range(pieces):
                at = q * piece_rows
                sink[t, m, at : at + piece_rows] = part_a[here_a ^ q, m]
                sink[t, m, vectors + at : vectors + at + piece_rows] = part_b[here_b ^ q, m]


def prepare(own, oth, columns, place):
    pieces, moms, piece_rows, vectors = own[0].shape
    vmem = pl.BlockSpec(memory_space=pltpu.VMEM)
    return pl.pallas_call(
        prepare_kernel,
        out_shape=(
            jax.ShapeDtypeStruct((2, 2 * moms * columns, 2 * vectors), BF16),
            jax.ShapeDtypeStruct((2, moms, 2 * vectors, vectors), BF16),
        ),
        in_specs=[pl.BlockSpec(memory_space=pltpu.SMEM)] + [vmem] * 4,
        out_specs=(vmem, vmem),
        compiler_params=params(),
        cost_estimate=cost(0, 16 * own[0].size),
        name="prepare",
    )(place, *own, *oth)


def dress_kernel(dists, chained, first_pair, place, other_src, other_snk, left, sink, *refs):
    count = len(dists)
    mine, near = refs[:count], refs[count : 2 * count]
    out, panel, done, sems = refs[2 * count + chained :]
    moms, width, vectors = sink.shape[1:]
    columns = out.shape[3]
    pair, last = pl.program_id(0), pl.num_programs(0) - 1
    x, z = place[X], place[Z]
    src, snk = other_src[pair], other_snk[pair]
    block = mine[0].shape[2]

    def store(k, of_pair):
        lanes = pl.ds(pl.multiple_of((z ^ dists[k]) * vectors, vectors), vectors)
        return pltpu.make_async_copy(done.at[k], out.at[of_pair + first_pair, :, :, :, lanes], sems.at[k])

    for k in range(count):
        at_mine = pl.ds(pl.multiple_of(k * vectors + x * block, block), block)
        at_near = pl.ds(pl.multiple_of(k * vectors + (1 - x) * block, block), block)
        for part in range(2):
            lanes = slice(part * vectors, (part + 1) * vectors)
            panel[at_mine, lanes] = mine[k][0, part]
            panel[at_near, lanes] = near[k][0, part]

    contract = (((1,), (1,)), ((), ()))
    right = lax.dot_general(left[src], panel[...], contract, preferred_element_type=F32).astype(BF16)
    for k in range(count):
        at = slice(k * vectors, (k + 1) * vectors)

        @pl.when(pair > 0)
        def _(k=k):
            store(k, pair - 1).wait()

        for m in range(moms):
            rows = right[2 * m * columns : 2 * (m + 1) * columns, at]
            both = lax.dot_general(rows, sink[snk, m], contract, preferred_element_type=F32)
            done[k, m, 0] = (both[:columns, :vectors] - both[columns:, vectors:]).astype(BF16)
            done[k, m, 1] = (both[:columns, vectors:] + both[columns:, :vectors]).astype(BF16)
        store(k, pair).start()

    @pl.when(pair == last)
    def _():
        for k in range(count):
            store(k, pair).wait()


def dress(out, out_shape, first_pair, pairs, dists, mine, near, left, sink, place, other_src, other_snk):
    _, _, block, vectors = mine[0][0].shape
    count = len(mine)
    moms = sink.shape[1]
    columns = out_shape.shape[3]
    whole = pl.BlockSpec(memory_space=pltpu.VMEM)
    chunks = [
        pl.BlockSpec((1, 2, block, vectors), lambda p, *_, first=first: (p + first, 0, 0, 0))
        for _, first in (*mine, *near)
    ]
    chained = out is not None
    operands = [left, sink, *(part for part, _ in (*mine, *near))] + ([out] if chained else [])
    in_specs = [whole, whole] + chunks + [pl.BlockSpec(memory_space=pl.ANY)] * chained
    macs = pairs * count * 2 * (2 * moms * columns) * (2 * vectors) * vectors
    return pl.pallas_call(
        functools.partial(dress_kernel, dists, chained, first_pair),
        out_shape=out_shape,
        grid_spec=pltpu.PrefetchScalarGridSpec(
            num_scalar_prefetch=3,
            grid=(pairs,),
            in_specs=in_specs,
            out_specs=pl.BlockSpec(memory_space=pl.ANY),
            scratch_shapes=[
                pltpu.VMEM((count * 2 * block, 2 * vectors), BF16),
                pltpu.VMEM((count, moms, 2, columns, vectors), BF16),
                pltpu.SemaphoreType.DMA((count,)),
            ],
        ),
        input_output_aliases={3 + len(operands) - 1: 0} if chained else {},
        compiler_params=params(1),
        cost_estimate=cost(2 * macs, 2**21),
        name="dress",
    )(place, other_src[first_pair : first_pair + pairs], other_snk[first_pair : first_pair + pairs], *operands)


CHUNKS = (1, 2, 2, 2)
HOOKS = [[], [('z', 3, 0)], [('x', 0, 0)], [], [('x', 3, 0), ('z', 1, 0)], [('z', 3, 1)], [('z', 2, 0), ('x', 1, 0), ('x', 3, 1)]]
CALLS = ((0, 2, (0, 1, 2, 3)), (2, 2, (0, 1, 2, 3)))
GATES = {}
AFTER = {}
FROM = {}


def exchange(value, axis, mask, among=lambda i: True):
    return lax.ppermute(value, axis, [(i, i ^ mask) for i in range(lax.axis_size(axis)) if among(i)])


def fast(eigvecs, momenta, pair_list, panels):
    vectors = eigvecs.shape[4]
    pair_count, _, rows, width = panels.shape
    moms = momenta.shape[0]
    space_count = lax.axis_size("space")
    spins = width // vectors
    space = lax.axis_index("space")
    tm = lax.axis_index("tm")
    x, z = space & 1, space >> 1
    low, high = z & 1, z >> 1
    place = jnp.stack(
        [space, x, z, low, high, x * 4 + low * 2 + high, low * 4 + x * 2 + high]
    ).astype(jnp.int32)
    other = (pair_list != tm).astype(jnp.int32)
    other_src, other_snk = other[:, 0], other[:, 1]

    factor = 1.0 / math.sqrt(6.0 * eigvecs.shape[3] * space_count * vectors)
    plan = [
        (d, c * (pair_count // n), pair_count // n) for d, n in enumerate(CHUNKS) for c in range(n)
    ]
    send_a, send_b, keep_a, keep_b = gram_halves(eigvecs[0], momenta, place, factor)
    blocks = cut_panels(panels, vectors, plan, CUT_VMEM, place)

    raw, held, steps = {}, {}, []

    def fetch(name):
        if name not in raw:
            hop, d, c = name
            value = blocks[d, c] if hop == "z" or d == 0 else fetch(("z", d, c))
            if name in FROM:
                value, _ = lax.optimization_barrier((value, steps[FROM[name]]))
            raw[name] = exchange(meet(value, AFTER.get(name)), "space", 2 * d if hop == "z" else 1)
        held.setdefault(name, raw[name])
        return raw[name]

    def meet(value, names):
        if not names:
            return value
        for name in names:
            fetch(name)
        value, *came = lax.optimization_barrier((value, *(held[name] for name in names)))
        held.update(zip(names, came))
        return value

    along_x, low_z, high_z = 1, 2, 4

    def step(*sends):
        came = [exchange(value, "space", mask) for value, mask in sends]
        came[0] = meet(came[0], HOOKS[len(steps)])
        steps.append(came[0])
        return came

    came = step((send_a, along_x), (send_b, low_z))
    send_a, send_b, keep_a, keep_b = fold(fold_kernel, keep_a, keep_b, *came, place)
    came = step((send_a, low_z), (send_b, along_x))
    send, keep = fold(join_kernel, keep_a, keep_b, *came, place)
    (came,) = step((send, high_z))
    field = (keep + came.astype(F32)).astype(BF16)[None]
    (came,) = step((field, high_z))
    field = jnp.concatenate([field, came], 0)
    parts = [field[..., :vectors], field[..., vectors:]]
    came = step((parts[0], low_z), (parts[1], along_x))
    parts = [jnp.concatenate([part, new], 0) for part, new in zip(parts, came)]
    came = step((parts[0], along_x), (parts[1], low_z))
    own = [jnp.concatenate([part, new], 0) for part, new in zip(parts, came)]
    oth = [exchange(part, "tm", 1) for part in own]
    oth[0] = meet(oth[0], HOOKS[6])

    columns = width // space_count
    out_shape = jax.ShapeDtypeStruct((pair_count, moms, 2, columns, width), BF16)

    def part(hop, d, first):
        c, at = divmod(first, pair_count // CHUNKS[d])
        if (hop, d) == ("z", 0):
            return blocks[0, c], at
        fetch((hop, d, c))
        return held[hop, d, c], at

    left, sink = prepare(own, oth, columns, place)
    out = None
    for call, (first, pairs, dists) in enumerate(CALLS):
        for _, d, c in GATES.get(call, ()):
            value, out = lax.optimization_barrier((fetch(("z", d, c)), out))
            raw["z", d, c] = held["z", d, c] = value
        mine = [part("z", d, first) for d in dists]
        near = [part("x", d, first) for d in dists]
        out = dress(
            out, out_shape, first, pairs, dists, mine, near, left, sink, place, other_src, other_snk
        )
    return out


def phased_block(cosine, sine_part, real_part, imag_part):
    cos_col = cosine[:, None]
    sin_col = sine_part[:, None]
    wave_re = cos_col * real_part + sin_col * imag_part
    wave_im = cos_col * imag_part - sin_col * real_part
    upper = jnp.concatenate([wave_re, wave_im], -1)
    lower = jnp.concatenate([wave_im, -wave_re], -1)
    return jnp.stack([upper, lower], -4).astype(jnp.bfloat16)


def general(eigvecs, momenta, pair_list, panels):
    slice_count, _, colors, slab_sites, vectors = eigvecs.shape
    mom_count = momenta.shape[0]
    space_count = lax.axis_size("space")
    first_site = lax.axis_index("space") * slab_sites
    site_index = first_site + jnp.arange(slab_sites, dtype=jnp.int32)
    xpos = site_index % LX
    ypos = site_index // LX % LX
    zpos = site_index // (LX * LX)
    wave = (
        momenta[:, 0:1] * xpos[None, :]
        + momenta[:, 1:2] * ypos[None, :]
        + momenta[:, 2:3] * zpos[None, :]
    )
    wave = jnp.mod(wave, LX)
    angle = wave.astype(jnp.float32) * jnp.float32(2.0 * math.pi / LX)
    cosine = jnp.cos(angle)
    sine_part = jnp.sin(angle)
    factor = 1.0 / math.sqrt(6.0 * slab_sites * space_count * vectors)
    real_part = eigvecs[:, 0].astype(jnp.float32)
    imag_part = eigvecs[:, 1].astype(jnp.float32)
    phased_all = jnp.concatenate(
        [
            phased_block(cosine[moment], sine_part[moment], real_part, imag_part)
            for moment in range(mom_count)
        ],
        -1,
    )
    phased_all = phased_all.reshape(slice_count, 2, colors, slab_sites, mom_count, 2 * vectors)
    gram_local = jnp.einsum(
        "trcsk,trcsml->tmkl", eigvecs, phased_all, preferred_element_type=jnp.float32
    )
    gram_local = factor * gram_local
    summed = lax.psum(gram_local, "space")
    own_fields = summed.astype(jnp.bfloat16)
    meson_fields = lax.all_gather(own_fields, "tm", axis=0, tiled=True)
    pair_count = pair_list.shape[0]
    panel_rows = panels.shape[2]
    panel_width = panels.shape[3]
    spins = panel_width // vectors
    source_fields = jnp.take(meson_fields, pair_list[:, 0], axis=0).reshape(
        pair_count, mom_count, vectors, 2, vectors
    )
    sink_fields = jnp.take(meson_fields, pair_list[:, 1], axis=0).reshape(
        pair_count, mom_count, vectors, 2, vectors
    )
    panel_parts = panels.reshape(pair_count, 2, panel_rows, spins, vectors)
    panel_re = panel_parts[:, 0]
    panel_im = panel_parts[:, 1]
    panel_mix = jnp.stack(
        [jnp.stack([panel_re, panel_im], 1), jnp.stack([panel_im, -panel_re], 1)], 1
    )
    right_dressed = jnp.einsum(
        "porxbk,pmlrk->pmoxbl", panel_mix, source_fields, preferred_element_type=jnp.float32
    )
    right_dressed = right_dressed.astype(jnp.bfloat16).reshape(
        pair_count * mom_count, 2, panel_rows, panel_width
    )
    turned = lax.all_to_all(right_dressed, "space", split_axis=3, concat_axis=2, tiled=True)
    column_count = turned.shape[3]
    turned = turned.reshape(pair_count, mom_count, 2, spins, vectors, column_count)
    turned_re = turned[:, :, 0]
    turned_im = turned[:, :, 1]
    mixed_parts = jnp.stack(
        [jnp.stack([turned_re, -turned_im], 2), jnp.stack([turned_im, turned_re], 2)], 2
    )
    dressed = jnp.einsum(
        "pmorajc,pmkrj->pmocak", mixed_parts, sink_fields, preferred_element_type=jnp.float32
    )
    return dressed.reshape(pair_count, mom_count, 2, column_count, panel_width).astype(jnp.bfloat16)


def local(eigvecs, momenta, pair_list, panels):
    slices, _, _, sites, vectors = eigvecs.shape
    pairs, _, rows, width = panels.shape
    space_count = lax.axis_size("space")
    spins = width // vectors
    fits = (
        slices == 1
        and lax.axis_size("tm") == 2
        and space_count == 2 * spins
        and spins == 4
        and rows * space_count == width
        and rows % 128 == 0
        and (vectors // space_count) % 16 == 0
        and sites % 16 == 0
        and pairs % 2 == 0
        and momenta.shape[0] <= 8
    )
    return (fast if fits else general)(eigvecs, momenta, pair_list, panels)


def solution(mesh):
    placed = (
        P(("cfg", "tm"), None, None, "space", None),
        P(),
        P("tm", None),
        P(("cfg", "tm"), None, "space", None),
    )
    return jax.shard_map(
        local,
        mesh=mesh,
        in_specs=placed,
        out_specs=P(("cfg", "tm"), None, None, "space", None),
        check_vma=False,
    )
```

```python
import functools
import math

import jax
import jax.numpy as jnp
from jax import lax
from jax.experimental import pallas as pl
from jax.experimental.pallas import tpu as pltpu
from jax.sharding import PartitionSpec as P

LX = 64
LX_BITS = LX.bit_length() - 1
F32, BF16 = jnp.float32, jnp.bfloat16
SPACE, X, Z, Z_LOW, Z_HIGH, HERE_A, HERE_B, MOMENTA = range(8)
VMEM_LIMIT = 24 * 1024 * 1024
CUT_VMEM = 24 * 1024 * 1024


def params(steps=0):
    return pltpu.CompilerParams(
        vmem_limit_bytes=VMEM_LIMIT, dimension_semantics=("arbitrary",) * steps or None
    )


def cost(flops, bytes_accessed):
    return pl.CostEstimate(flops=int(flops), bytes_accessed=int(bytes_accessed), transcendentals=0)


def gram_kernel(factor, place, eig, send_a, send_b, keep_a, keep_b, phased, total):
    colors, sites, vectors = eig.shape[1:]
    moms, half = send_a.shape[:2]
    site = place[SPACE] * sites + lax.broadcasted_iota(jnp.int32, (sites, 128), 0)
    lane = lax.broadcasted_iota(jnp.int32, (sites, 128), 1)
    coords = (site & (LX - 1), (site >> LX_BITS) & (LX - 1), site >> (2 * LX_BITS))
    wave = jnp.zeros((sites, 128), jnp.int32)
    for m in range(moms):
        mine = sum(place[MOMENTA + 3 * m + j] * coords[j] for j in range(3))
        wave = jnp.where(lane == m, mine, wave)
    angle = (wave & (LX - 1)).astype(F32) * F32(2.0 * math.pi / LX)
    cosine, sine = jnp.cos(angle), jnp.sin(angle)
    rows = colors * sites
    both = eig[...].reshape(2 * rows, vectors)
    for m in range(moms):
        c, s = cosine[:, m : m + 1], sine[:, m : m + 1]
        for color in range(colors):
            re, im = eig[0, color].astype(F32), eig[1, color].astype(F32)
            wave_re, wave_im = c * re + s * im, c * im - s * re
            at = color * sites
            phased[at : at + sites, :vectors] = wave_re.astype(BF16)
            phased[at : at + sites, vectors:] = wave_im.astype(BF16)
            at += rows
            phased[at : at + sites, :vectors] = wave_im.astype(BF16)
            phased[at : at + sites, vectors:] = (-wave_re).astype(BF16)
        total[...] = factor * lax.dot_general(
            both, phased[...], (((0,), (0,)), ((), ())), preferred_element_type=F32
        )
        for send, keep, bit, lanes in (
            (send_a, keep_a, place[X], slice(None, vectors)),
            (send_b, keep_b, place[Z_LOW], slice(vectors, None)),
        ):
            send[m] = total[pl.ds(pl.multiple_of((1 - bit) * half, half), half), lanes].astype(BF16)
            keep[m] = total[pl.ds(pl.multiple_of(bit * half, half), half), lanes]


def gram_halves(eig, moms, place, factor):
    _, colors, sites, vectors = eig.shape
    shape = (moms, vectors // 2, vectors)
    smem = pl.BlockSpec(memory_space=pltpu.SMEM)
    vmem = pl.BlockSpec(memory_space=pltpu.VMEM)
    return pl.pallas_call(
        functools.partial(gram_kernel, factor),
        out_shape=[jax.ShapeDtypeStruct(shape, kind) for kind in (BF16, BF16, F32, F32)],
        in_specs=[smem, vmem],
        out_specs=[vmem] * 4,
        scratch_shapes=[
            pltpu.VMEM((2 * colors * sites, 2 * vectors), BF16),
            pltpu.VMEM((vectors, 2 * vectors), F32),
        ],
        compiler_params=params(),
        cost_estimate=cost(4 * colors * sites * vectors * moms * 2 * vectors, 3 * 2**20),
        name="gram",
    )(place, eig)


def cut_kernel(plan, place, panels, *refs):
    cuts, sems = refs[:-1], refs[-1]
    vectors = cuts[0].shape[3]
    copies = []
    for i, (d, first, _) in enumerate(plan):
        lanes = pl.ds(pl.multiple_of((place[Z] ^ d) * vectors, vectors), vectors)
        source = panels.at[first : first + cuts[i].shape[0], :, :, lanes]
        copies.append(pltpu.make_async_copy(source, cuts[i], sems.at[i]))
        copies[-1].start()
    for copy in copies:
        copy.wait()


def cut_panels(panels, vectors, plan, vmem, place):
    cuts = pl.pallas_call(
        functools.partial(cut_kernel, plan),
        out_shape=[jax.ShapeDtypeStruct((size, *panels.shape[1:3], vectors), BF16) for _, _, size in plan],
        in_specs=[pl.BlockSpec(memory_space=pltpu.SMEM), pl.BlockSpec(memory_space=pl.ANY)],
        out_specs=[pl.BlockSpec(memory_space=pltpu.VMEM)] * len(plan),
        scratch_shapes=[pltpu.SemaphoreType.DMA((len(plan),))],
        compiler_params=pltpu.CompilerParams(vmem_limit_bytes=vmem),
        cost_estimate=cost(0, 4 * panels.size),
        name="cut",
    )(place, panels)
    return {(d, first // size): cut for (d, first, size), cut in zip(plan, cuts)}


def fold_kernel(place, keep_a, keep_b, came_a, came_b, send_a, send_b, left_a, left_b):
    half = send_a.shape[1]
    for keep, came, bit, send, left in (
        (keep_a, came_a, place[Z_LOW], send_a, left_a),
        (keep_b, came_b, place[X], send_b, left_b),
    ):
        own = pl.ds(pl.multiple_of(bit * half, half), half)
        off = pl.ds(pl.multiple_of((1 - bit) * half, half), half)
        left[...] = keep[:, own, :] + came[:, own, :].astype(F32)
        send[...] = (keep[:, off, :] + came[:, off, :].astype(F32)).astype(BF16)


def join_kernel(place, keep_a, keep_b, came_a, came_b, send, left):
    half, width = send.shape[1:]
    bit = place[Z_HIGH]
    own = pl.ds(pl.multiple_of(bit * half, half), half)
    off = pl.ds(pl.multiple_of((1 - bit) * half, half), half)
    for keep, came, lanes in (
        (keep_a, came_a, slice(None, width // 2)),
        (keep_b, came_b, slice(width // 2, None)),
    ):
        left[:, :, lanes] = keep[:, own, :] + came[:, own, :].astype(F32)
        send[:, :, lanes] = (keep[:, off, :] + came[:, off, :].astype(F32)).astype(BF16)


def fold(kernel, keep_a, keep_b, came_a, came_b, place):
    moms, rows, width = keep_a.shape
    if kernel is join_kernel:
        shape, kinds = (moms, rows // 2, 2 * width), (BF16, F32)
    else:
        shape, kinds = (moms, rows // 2, width), (BF16, BF16, F32, F32)
    vmem = pl.BlockSpec(memory_space=pltpu.VMEM)
    return pl.pallas_call(
        kernel,
        out_shape=[jax.ShapeDtypeStruct(shape, kind) for kind in kinds],
        in_specs=[pl.BlockSpec(memory_space=pltpu.SMEM)] + [vmem] * 4,
        out_specs=[vmem] * len(kinds),
        compiler_params=params(),
        cost_estimate=cost(2 * keep_a.size, 16 * keep_a.size),
        name="fold",
    )(place, keep_a, keep_b, came_a, came_b)


def halve_kernel(field, came, part_a, part_b, both):
    vectors = part_a.shape[3]
    for i, piece in enumerate((field, came)):
        for j, part in enumerate((part_a, part_b)):
            value = piece[0, :, :, j * vectors : (j + 1) * vectors]
            part[i] = value
            both[j, i] = value


def pair_kernel(own_a, own_b, came_a, came_b, part_a, part_b, both):
    count = own_a.shape[0]
    for j, (own, came, part) in enumerate(((own_a, came_a, part_a), (own_b, came_b, part_b))):
        part[:count] = own[...]
        part[count:] = came[...]
        both[j] = came[...]


def both_kernel(came_a, came_b, both):
    both[0] = came_a[...]
    both[1] = came_b[...]


def gather(kernel, *pieces):
    count, moms, rows, width = pieces[0].shape
    shapes = {
        halve_kernel: [(2 * count, moms, rows, width // 2)] * 2 + [(2, 2 * count, moms, rows, width // 2)],
        pair_kernel: [(2 * count, moms, rows, width)] * 2 + [(2, count, moms, rows, width)],
        both_kernel: [(2, count, moms, rows, width)],
    }[kernel]
    vmem = pl.BlockSpec(memory_space=pltpu.VMEM)
    return pl.pallas_call(
        kernel,
        out_shape=[jax.ShapeDtypeStruct(shape, BF16) for shape in shapes],
        in_specs=[vmem] * len(pieces),
        out_specs=[vmem] * len(shapes),
        compiler_params=params(),
        cost_estimate=cost(0, 4 * len(pieces) * pieces[0].size),
        name="gather",
    )(*pieces)


def prepare_kernel(groups, place, *refs):
    fields, (left, sink) = refs[:-2], refs[-2:]
    moms, piece_rows, vectors = fields[0].shape[2:]
    columns = left.shape[1] // (2 * moms)
    per = columns // piece_rows
    x = place[X]
    for t in range(2):
        for p, here in enumerate((place[HERE_A], place[HERE_B])):
            j = 0
            for field in fields[t * groups : (t + 1) * groups]:
                for i in range(field.shape[1]):
                    q = here ^ j
                    j += 1
                    to_sink = pl.ds(pl.multiple_of(p * vectors + q * piece_rows, piece_rows), piece_rows)
                    for m in range(moms):
                        sink[t, m, to_sink] = field[p, i, m]

                    @pl.when(q // per == x)
                    def _(field=field, i=i, q=q):
                        for m in range(moms):
                            rows = field[p, i, m]
                            at = pl.multiple_of(2 * m * columns + (q - x * per) * piece_rows, piece_rows)
                            up, down = pl.ds(at, piece_rows), pl.ds(at + columns, piece_rows)
                            if p == 0:
                                left[t, up, :vectors] = rows
                                left[t, down, vectors:] = rows
                            else:
                                left[t, up, vectors:] = rows
                                left[t, down, :vectors] = -rows


def prepare(own, oth, columns, place):
    moms, piece_rows, vectors = own[0].shape[2:]
    vmem = pl.BlockSpec(memory_space=pltpu.VMEM)
    return pl.pallas_call(
        functools.partial(prepare_kernel, len(own)),
        out_shape=(
            jax.ShapeDtypeStruct((2, 2 * moms * columns, 2 * vectors), BF16),
            jax.ShapeDtypeStruct((2, moms, 2 * vectors, vectors), BF16),
        ),
        in_specs=[pl.BlockSpec(memory_space=pltpu.SMEM)] + [vmem] * (len(own) + len(oth)),
        out_specs=(vmem, vmem),
        compiler_params=params(),
        cost_estimate=cost(0, 16 * own[-1].size),
        name="prepare",
    )(place, *own, *oth)


def dress_kernel(dists, chained, first_pair, place, other_src, other_snk, left, sink, *refs):
    count = len(dists)
    mine, near = refs[:count], refs[count : 2 * count]
    out, panel, done, sems = refs[2 * count + chained :]
    moms, width, vectors = sink.shape[1:]
    columns = out.shape[3]
    pair, last = pl.program_id(0), pl.num_programs(0) - 1
    x, z = place[X], place[Z]
    src, snk = other_src[pair], other_snk[pair]
    block = mine[0].shape[2]

    def store(k, of_pair):
        lanes = pl.ds(pl.multiple_of((z ^ dists[k]) * vectors, vectors), vectors)
        return pltpu.make_async_copy(done.at[k], out.at[of_pair + first_pair, :, :, :, lanes], sems.at[k])

    for k in range(count):
        at_mine = pl.ds(pl.multiple_of(k * vectors + x * block, block), block)
        at_near = pl.ds(pl.multiple_of(k * vectors + (1 - x) * block, block), block)
        for part in range(2):
            lanes = slice(part * vectors, (part + 1) * vectors)
            panel[at_mine, lanes] = mine[k][0, part]
            panel[at_near, lanes] = near[k][0, part]

    contract = (((1,), (1,)), ((), ()))
    right = lax.dot_general(left[src], panel[...], contract, preferred_element_type=F32).astype(BF16)

    @pl.when(pair > 0)
    def _():
        for k in range(count):
            store(k, pair - 1).wait()

    for m in range(moms):
        part = right[2 * m * columns : 2 * (m + 1) * columns]
        rows = jnp.concatenate([part[:, k * vectors : (k + 1) * vectors] for k in range(count)], 0)
        both = lax.dot_general(rows, sink[snk, m], contract, preferred_element_type=F32)
        for k in range(count):
            re = both[2 * k * columns : (2 * k + 1) * columns]
            im = both[(2 * k + 1) * columns : (2 * k + 2) * columns]
            done[k, m, 0] = (re[:, :vectors] - im[:, vectors:]).astype(BF16)
            done[k, m, 1] = (re[:, vectors:] + im[:, :vectors]).astype(BF16)
    for k in range(count):
        store(k, pair).start()

    @pl.when(pair == last)
    def _():
        for k in range(count):
            store(k, pair).wait()


def dress(out, out_shape, first_pair, pairs, dists, mine, near, left, sink, place, other_src, other_snk):
    _, _, block, vectors = mine[0][0].shape
    count = len(mine)
    moms = sink.shape[1]
    columns = out_shape.shape[3]
    whole = pl.BlockSpec(memory_space=pltpu.VMEM)
    chunks = [
        pl.BlockSpec((1, 2, block, vectors), lambda p, *_, first=first: (p + first, 0, 0, 0))
        for _, first in (*mine, *near)
    ]
    chained = out is not None
    operands = [left, sink, *(part for part, _ in (*mine, *near))] + ([out] if chained else [])
    in_specs = [whole, whole] + chunks + [pl.BlockSpec(memory_space=pl.ANY)] * chained
    macs = pairs * count * 2 * (2 * moms * columns) * (2 * vectors) * vectors
    return pl.pallas_call(
        functools.partial(dress_kernel, dists, chained, first_pair),
        out_shape=out_shape,
        grid_spec=pltpu.PrefetchScalarGridSpec(
            num_scalar_prefetch=3,
            grid=(pairs,),
            in_specs=in_specs,
            out_specs=pl.BlockSpec(memory_space=pl.ANY),
            scratch_shapes=[
                pltpu.VMEM((count * 2 * block, 2 * vectors), BF16),
                pltpu.VMEM((count, moms, 2, columns, vectors), BF16),
                pltpu.SemaphoreType.DMA((count,)),
            ],
        ),
        input_output_aliases={3 + len(operands) - 1: 0} if chained else {},
        compiler_params=params(1),
        cost_estimate=cost(2 * macs, 2**21),
        name="dress",
    )(place, other_src[first_pair : first_pair + pairs], other_snk[first_pair : first_pair + pairs], *operands)


CHUNKS = (1, 2, 2, 2)
HOOKS = [[], [('z', 3, 0)], [], [('x', 0, 0)], [('x', 3, 0), ('z', 1, 0)], [('z', 3, 1)], [('z', 2, 0), ('x', 1, 0), ('x', 3, 1), ('z', 1, 1)]]
LOCK = (False, False)
CALLS = ((0, 2, (0, 1, 2, 3)), (2, 2, (0, 1, 3)), (2, 2, (2,)))
GATES = {1: [('x', 2, 1)]}
AFTER = {}
FROM = {('z', 2, 1): 5}


def exchange(value, axis, mask, among=lambda i: True):
    return lax.ppermute(value, axis, [(i, i ^ mask) for i in range(lax.axis_size(axis)) if among(i)])


def fast(eigvecs, momenta, pair_list, panels):
    vectors = eigvecs.shape[4]
    pair_count, _, rows, width = panels.shape
    moms = momenta.shape[0]
    space_count = lax.axis_size("space")
    spins = width // vectors
    space = lax.axis_index("space")
    tm = lax.axis_index("tm")
    x, z = space & 1, space >> 1
    low, high = z & 1, z >> 1
    where = [space, x, z, low, high, x * 4 + low * 2 + high, low * 4 + x * 2 + high]
    place = jnp.stack([value.astype(jnp.int32) for value in (*where, *momenta.reshape(-1))])
    other = (pair_list != tm).astype(jnp.int32)
    other_src, other_snk = other[:, 0], other[:, 1]

    factor = 1.0 / math.sqrt(6.0 * eigvecs.shape[3] * space_count * vectors)
    plan = [
        (d, c * (pair_count // n), pair_count // n) for d, n in enumerate(CHUNKS) for c in range(n)
    ]
    send_a, send_b, keep_a, keep_b = gram_halves(eigvecs[0], moms, place, factor)
    blocks = cut_panels(panels, vectors, plan, CUT_VMEM, place)

    raw, held, steps = {}, {}, []

    def fetch(name):
        if name not in raw:
            hop, d, c = name
            value = blocks[d, c] if hop == "z" or d == 0 else fetch(("z", d, c))
            if name in FROM:
                value, _ = lax.optimization_barrier((value, steps[FROM[name]]))
            raw[name] = exchange(meet(value, AFTER.get(name)), "space", 2 * d if hop == "z" else 1)
        held.setdefault(name, raw[name])
        return raw[name]

    def meet(value, names):
        if not names:
            return value
        for name in names:
            fetch(name)
        value, *came = lax.optimization_barrier((value, *(held[name] for name in names)))
        held.update(zip(names, came))
        return value

    along_x, low_z, high_z = 1, 2, 4

    def step(*sends):
        came = [exchange(value, "space", mask) for value, mask in sends]
        came[0] = meet(came[0], HOOKS[len(steps)])
        steps.append(came[0])
        return came

    came = step((send_a, along_x), (send_b, low_z))
    send_a, send_b, keep_a, keep_b = fold(fold_kernel, keep_a, keep_b, *came, place)
    came = step((send_a, low_z), (send_b, along_x))
    send, keep = fold(join_kernel, keep_a, keep_b, *came, place)
    (came,) = step((send, high_z))
    field = (keep + came.astype(F32)).astype(BF16)[None]
    (came,) = step((field, high_z))
    own, oth = [], []

    def share(both):
        own.append(both)
        oth.append(exchange(both, "tm", 1))

    def after_share(value, count):
        if len(oth) >= count:
            value, oth[count - 1] = lax.optimization_barrier((value, oth[count - 1]))
        return value

    *parts, both = gather(halve_kernel, field, came)
    share(both)
    came = step((parts[0], low_z), (parts[1], along_x))
    if LOCK[0]:
        came[0] = after_share(came[0], 1)
    *parts, both = gather(pair_kernel, *parts, *came)
    share(both)
    came = step((parts[0], along_x), (parts[1], low_z))
    if LOCK[1]:
        came[0] = after_share(came[0], 2)
    share(*gather(both_kernel, *came))
    oth[2] = meet(oth[2], HOOKS[6])

    columns = width // space_count
    out_shape = jax.ShapeDtypeStruct((pair_count, moms, 2, columns, width), BF16)

    def part(hop, d, first):
        c, at = divmod(first, pair_count // CHUNKS[d])
        if (hop, d) == ("z", 0):
            return blocks[0, c], at
        fetch((hop, d, c))
        return held[hop, d, c], at

    left, sink = prepare(own, oth, columns, place)
    out = None
    for call, (first, pairs, dists) in enumerate(CALLS):
        for _, d, c in GATES.get(call, ()):
            value, out = lax.optimization_barrier((fetch(("z", d, c)), out))
            raw["z", d, c] = held["z", d, c] = value
        mine = [part("z", d, first) for d in dists]
        near = [part("x", d, first) for d in dists]
        out = dress(
            out, out_shape, first, pairs, dists, mine, near, left, sink, place, other_src, other_snk
        )
    return out


def phased_block(cosine, sine_part, real_part, imag_part):
    cos_col = cosine[:, None]
    sin_col = sine_part[:, None]
    wave_re = cos_col * real_part + sin_col * imag_part
    wave_im = cos_col * imag_part - sin_col * real_part
    upper = jnp.concatenate([wave_re, wave_im], -1)
    lower = jnp.concatenate([wave_im, -wave_re], -1)
    return jnp.stack([upper, lower], -4).astype(jnp.bfloat16)


def general(eigvecs, momenta, pair_list, panels):
    slice_count, _, colors, slab_sites, vectors = eigvecs.shape
    mom_count = momenta.shape[0]
    space_count = lax.axis_size("space")
    first_site = lax.axis_index("space") * slab_sites
    site_index = first_site + jnp.arange(slab_sites, dtype=jnp.int32)
    xpos = site_index % LX
    ypos = site_index // LX % LX
    zpos = site_index // (LX * LX)
    wave = (
        momenta[:, 0:1] * xpos[None, :]
        + momenta[:, 1:2] * ypos[None, :]
        + momenta[:, 2:3] * zpos[None, :]
    )
    wave = jnp.mod(wave, LX)
    angle = wave.astype(jnp.float32) * jnp.float32(2.0 * math.pi / LX)
    cosine = jnp.cos(angle)
    sine_part = jnp.sin(angle)
    factor = 1.0 / math.sqrt(6.0 * slab_sites * space_count * vectors)
    real_part = eigvecs[:, 0].astype(jnp.float32)
    imag_part = eigvecs[:, 1].astype(jnp.float32)
    phased_all = jnp.concatenate(
        [
            phased_block(cosine[moment], sine_part[moment], real_part, imag_part)
            for moment in range(mom_count)
        ],
        -1,
    )
    phased_all = phased_all.reshape(slice_count, 2, colors, slab_sites, mom_count, 2 * vectors)
    gram_local = jnp.einsum(
        "trcsk,trcsml->tmkl", eigvecs, phased_all, preferred_element_type=jnp.float32
    )
    gram_local = factor * gram_local
    summed = lax.psum(gram_local, "space")
    own_fields = summed.astype(jnp.bfloat16)
    meson_fields = lax.all_gather(own_fields, "tm", axis=0, tiled=True)
    pair_count = pair_list.shape[0]
    panel_rows = panels.shape[2]
    panel_width = panels.shape[3]
    spins = panel_width // vectors
    source_fields = jnp.take(meson_fields, pair_list[:, 0], axis=0).reshape(
        pair_count, mom_count, vectors, 2, vectors
    )
    sink_fields = jnp.take(meson_fields, pair_list[:, 1], axis=0).reshape(
        pair_count, mom_count, vectors, 2, vectors
    )
    panel_parts = panels.reshape(pair_count, 2, panel_rows, spins, vectors)
    panel_re = panel_parts[:, 0]
    panel_im = panel_parts[:, 1]
    panel_mix = jnp.stack(
        [jnp.stack([panel_re, panel_im], 1), jnp.stack([panel_im, -panel_re], 1)], 1
    )
    right_dressed = jnp.einsum(
        "porxbk,pmlrk->pmoxbl", panel_mix, source_fields, preferred_element_type=jnp.float32
    )
    right_dressed = right_dressed.astype(jnp.bfloat16).reshape(
        pair_count * mom_count, 2, panel_rows, panel_width
    )
    turned = lax.all_to_all(right_dressed, "space", split_axis=3, concat_axis=2, tiled=True)
    column_count = turned.shape[3]
    turned = turned.reshape(pair_count, mom_count, 2, spins, vectors, column_count)
    turned_re = turned[:, :, 0]
    turned_im = turned[:, :, 1]
    mixed_parts = jnp.stack(
        [jnp.stack([turned_re, -turned_im], 2), jnp.stack([turned_im, turned_re], 2)], 2
    )
    dressed = jnp.einsum(
        "pmorajc,pmkrj->pmocak", mixed_parts, sink_fields, preferred_element_type=jnp.float32
    )
    return dressed.reshape(pair_count, mom_count, 2, column_count, panel_width).astype(jnp.bfloat16)


def local(eigvecs, momenta, pair_list, panels):
    slices, _, _, sites, vectors = eigvecs.shape
    pairs, _, rows, width = panels.shape
    space_count = lax.axis_size("space")
    spins = width // vectors
    fits = (
        slices == 1
        and lax.axis_size("tm") == 2
        and space_count == 2 * spins
        and spins == 4
        and rows * space_count == width
        and rows % 128 == 0
        and (vectors // space_count) % 16 == 0
        and sites % 16 == 0
        and pairs % 2 == 0
        and momenta.shape[0] <= 8
    )
    return (fast if fits else general)(eigvecs, momenta, pair_list, panels)


def solution(mesh):
    placed = (
        P(("cfg", "tm"), None, None, "space", None),
        P(),
        P("tm", None),
        P(("cfg", "tm"), None, "space", None),
    )
    return jax.shard_map(
        local,
        mesh=mesh,
        in_specs=placed,
        out_specs=P(("cfg", "tm"), None, None, "space", None),
        check_vma=False,
    )
```

```python
import functools
import math

import jax
import jax.numpy as jnp
from jax import lax
from jax.experimental import pallas as pl
from jax.experimental.pallas import tpu as pltpu
from jax.sharding import PartitionSpec as P

LX = 64
LX_BITS = LX.bit_length() - 1
F32, BF16 = jnp.float32, jnp.bfloat16
SPACE, X, Z, Z_LOW, Z_HIGH, HERE_A, HERE_B, MOMENTA = range(8)
VMEM_LIMIT = 24 * 1024 * 1024
CUT_VMEM = 24 * 1024 * 1024


def params(steps=0):
    return pltpu.CompilerParams(
        vmem_limit_bytes=VMEM_LIMIT, dimension_semantics=("arbitrary",) * steps or None
    )


def cost(flops, bytes_accessed):
    return pl.CostEstimate(flops=int(flops), bytes_accessed=int(bytes_accessed), transcendentals=0)


def gram_kernel(factor, place, eig, send_a, send_b, keep_a, keep_b, phased, total):
    colors, sites, vectors = eig.shape[1:]
    moms, half = send_a.shape[:2]
    site = place[SPACE] * sites + lax.broadcasted_iota(jnp.int32, (sites, 128), 0)
    lane = lax.broadcasted_iota(jnp.int32, (sites, 128), 1)
    coords = (site & (LX - 1), (site >> LX_BITS) & (LX - 1), site >> (2 * LX_BITS))
    wave = jnp.zeros((sites, 128), jnp.int32)
    for m in range(moms):
        mine = sum(place[MOMENTA + 3 * m + j] * coords[j] for j in range(3))
        wave = jnp.where(lane == m, mine, wave)
    angle = (wave & (LX - 1)).astype(F32) * F32(2.0 * math.pi / LX)
    cosine, sine = jnp.cos(angle), jnp.sin(angle)
    rows = colors * sites
    both = eig[...].reshape(2 * rows, vectors)
    for m in range(moms):
        c, s = cosine[:, m : m + 1], sine[:, m : m + 1]
        for color in range(colors):
            re, im = eig[0, color].astype(F32), eig[1, color].astype(F32)
            wave_re, wave_im = c * re + s * im, c * im - s * re
            at = color * sites
            phased[at : at + sites, :vectors] = wave_re.astype(BF16)
            phased[at : at + sites, vectors:] = wave_im.astype(BF16)
            at += rows
            phased[at : at + sites, :vectors] = wave_im.astype(BF16)
            phased[at : at + sites, vectors:] = (-wave_re).astype(BF16)
        total[...] = factor * lax.dot_general(
            both, phased[...], (((0,), (0,)), ((), ())), preferred_element_type=F32
        )
        for send, keep, bit, lanes in (
            (send_a, keep_a, place[X], slice(None, vectors)),
            (send_b, keep_b, place[Z_LOW], slice(vectors, None)),
        ):
            send[m] = total[pl.ds(pl.multiple_of((1 - bit) * half, half), half), lanes].astype(BF16)
            keep[m] = total[pl.ds(pl.multiple_of(bit * half, half), half), lanes]


def gram_halves(eig, moms, place, factor):
    _, colors, sites, vectors = eig.shape
    shape = (moms, vectors // 2, vectors)
    smem = pl.BlockSpec(memory_space=pltpu.SMEM)
    vmem = pl.BlockSpec(memory_space=pltpu.VMEM)
    return pl.pallas_call(
        functools.partial(gram_kernel, factor),
        out_shape=[jax.ShapeDtypeStruct(shape, kind) for kind in (BF16, BF16, F32, F32)],
        in_specs=[smem, vmem],
        out_specs=[vmem] * 4,
        scratch_shapes=[
            pltpu.VMEM((2 * colors * sites, 2 * vectors), BF16),
            pltpu.VMEM((vectors, 2 * vectors), F32),
        ],
        compiler_params=params(),
        cost_estimate=cost(4 * colors * sites * vectors * moms * 2 * vectors, 3 * 2**20),
        name="gram",
    )(place, eig)


def cut_kernel(plan, place, panels, *refs):
    cuts, sems = refs[:-1], refs[-1]
    vectors = cuts[0].shape[3]
    copies = []
    for i, (d, first, _) in enumerate(plan):
        lanes = pl.ds(pl.multiple_of((place[Z] ^ d) * vectors, vectors), vectors)
        source = panels.at[first : first + cuts[i].shape[0], :, :, lanes]
        copies.append(pltpu.make_async_copy(source, cuts[i], sems.at[i]))
        copies[-1].start()
    for copy in copies:
        copy.wait()


def cut_panels(panels, vectors, plan, vmem, place):
    cuts = pl.pallas_call(
        functools.partial(cut_kernel, plan),
        out_shape=[jax.ShapeDtypeStruct((size, *panels.shape[1:3], vectors), BF16) for _, _, size in plan],
        in_specs=[pl.BlockSpec(memory_space=pltpu.SMEM), pl.BlockSpec(memory_space=pl.ANY)],
        out_specs=[pl.BlockSpec(memory_space=pltpu.VMEM)] * len(plan),
        scratch_shapes=[pltpu.SemaphoreType.DMA((len(plan),))],
        compiler_params=pltpu.CompilerParams(vmem_limit_bytes=vmem),
        cost_estimate=cost(0, 4 * panels.size),
        name="cut",
    )(place, panels)
    return {(d, first // size): cut for (d, first, size), cut in zip(plan, cuts)}


def fold_kernel(place, keep_a, keep_b, came_a, came_b, send_a, send_b, left_a, left_b):
    half = send_a.shape[1]
    for keep, came, bit, send, left in (
        (keep_a, came_a, place[Z_LOW], send_a, left_a),
        (keep_b, came_b, place[X], send_b, left_b),
    ):
        own = pl.ds(pl.multiple_of(bit * half, half), half)
        off = pl.ds(pl.multiple_of((1 - bit) * half, half), half)
        left[...] = keep[:, own, :] + came[:, own, :].astype(F32)
        send[...] = (keep[:, off, :] + came[:, off, :].astype(F32)).astype(BF16)


def join_kernel(place, keep_a, keep_b, came_a, came_b, send, left):
    half, width = send.shape[1:]
    bit = place[Z_HIGH]
    own = pl.ds(pl.multiple_of(bit * half, half), half)
    off = pl.ds(pl.multiple_of((1 - bit) * half, half), half)
    for keep, came, lanes in (
        (keep_a, came_a, slice(None, width // 2)),
        (keep_b, came_b, slice(width // 2, None)),
    ):
        left[:, :, lanes] = keep[:, own, :] + came[:, own, :].astype(F32)
        send[:, :, lanes] = (keep[:, off, :] + came[:, off, :].astype(F32)).astype(BF16)


def fold(kernel, keep_a, keep_b, came_a, came_b, place):
    moms, rows, width = keep_a.shape
    if kernel is join_kernel:
        shape, kinds = (moms, rows // 2, 2 * width), (BF16, F32)
    else:
        shape, kinds = (moms, rows // 2, width), (BF16, BF16, F32, F32)
    vmem = pl.BlockSpec(memory_space=pltpu.VMEM)
    return pl.pallas_call(
        kernel,
        out_shape=[jax.ShapeDtypeStruct(shape, kind) for kind in kinds],
        in_specs=[pl.BlockSpec(memory_space=pltpu.SMEM)] + [vmem] * 4,
        out_specs=[vmem] * len(kinds),
        compiler_params=params(),
        cost_estimate=cost(2 * keep_a.size, 16 * keep_a.size),
        name="fold",
    )(place, keep_a, keep_b, came_a, came_b)


def halve_kernel(field, came, part_a, part_b, both):
    vectors = part_a.shape[3]
    for i, piece in enumerate((field, came)):
        for j, part in enumerate((part_a, part_b)):
            value = piece[0, :, :, j * vectors : (j + 1) * vectors]
            part[i] = value
            both[j, i] = value


def pair_kernel(own_a, own_b, came_a, came_b, part_a, part_b, both):
    count = own_a.shape[0]
    for j, (own, came, part) in enumerate(((own_a, came_a, part_a), (own_b, came_b, part_b))):
        part[:count] = own[...]
        part[count:] = came[...]
        both[j] = came[...]


def both_kernel(came_a, came_b, both):
    both[0] = came_a[...]
    both[1] = came_b[...]


def gather(kernel, *pieces):
    count, moms, rows, width = pieces[0].shape
    shapes = {
        halve_kernel: [(2 * count, moms, rows, width // 2)] * 2 + [(2, 2 * count, moms, rows, width // 2)],
        pair_kernel: [(2 * count, moms, rows, width)] * 2 + [(2, count, moms, rows, width)],
        both_kernel: [(2, count, moms, rows, width)],
    }[kernel]
    vmem = pl.BlockSpec(memory_space=pltpu.VMEM)
    return pl.pallas_call(
        kernel,
        out_shape=[jax.ShapeDtypeStruct(shape, BF16) for shape in shapes],
        in_specs=[vmem] * len(pieces),
        out_specs=[vmem] * len(shapes),
        compiler_params=params(),
        cost_estimate=cost(0, 4 * len(pieces) * pieces[0].size),
        name="gather",
    )(*pieces)


def prepare_kernel(groups, place, *refs):
    fields, (left, sink) = refs[:-2], refs[-2:]
    moms, piece_rows, vectors = fields[0].shape[2:]
    columns = left.shape[1] // (2 * moms)
    per = columns // piece_rows
    x = place[X]
    for t in range(2):
        for p, here in enumerate((place[HERE_A], place[HERE_B])):
            j = 0
            for field in fields[t * groups : (t + 1) * groups]:
                for i in range(field.shape[1]):
                    q = here ^ j
                    j += 1
                    to_sink = pl.ds(pl.multiple_of(p * vectors + q * piece_rows, piece_rows), piece_rows)
                    for m in range(moms):
                        sink[t, m, to_sink] = field[p, i, m]

                    @pl.when(q // per == x)
                    def _(field=field, i=i, q=q):
                        for m in range(moms):
                            rows = field[p, i, m]
                            at = pl.multiple_of(2 * m * columns + (q - x * per) * piece_rows, piece_rows)
                            up, down = pl.ds(at, piece_rows), pl.ds(at + columns, piece_rows)
                            if p == 0:
                                left[t, up, :vectors] = rows
                                left[t, down, vectors:] = rows
                            else:
                                left[t, up, vectors:] = rows
                                left[t, down, :vectors] = -rows


def prepare(own, oth, columns, place):
    moms, piece_rows, vectors = own[0].shape[2:]
    vmem = pl.BlockSpec(memory_space=pltpu.VMEM)
    return pl.pallas_call(
        functools.partial(prepare_kernel, len(own)),
        out_shape=(
            jax.ShapeDtypeStruct((2, 2 * moms * columns, 2 * vectors), BF16),
            jax.ShapeDtypeStruct((2, moms, 2 * vectors, vectors), BF16),
        ),
        in_specs=[pl.BlockSpec(memory_space=pltpu.SMEM)] + [vmem] * (len(own) + len(oth)),
        out_specs=(vmem, vmem),
        compiler_params=params(),
        cost_estimate=cost(0, 16 * own[-1].size),
        name="prepare",
    )(place, *own, *oth)


def dress_kernel(dists, chained, first_pair, place, other_src, other_snk, left, sink, *refs):
    count = len(dists)
    mine, near = refs[:count], refs[count : 2 * count]
    out, panel, done, sems = refs[2 * count + chained :]
    moms, width, vectors = sink.shape[1:]
    columns = out.shape[3]
    pair, last = pl.program_id(0), pl.num_programs(0) - 1
    x, z = place[X], place[Z]
    src, snk = other_src[pair], other_snk[pair]
    block = mine[0].shape[2]

    def store(k, of_pair):
        lanes = pl.ds(pl.multiple_of((z ^ dists[k]) * vectors, vectors), vectors)
        return pltpu.make_async_copy(done.at[k], out.at[of_pair + first_pair, :, :, :, lanes], sems.at[k])

    for k in range(count):
        at_mine = pl.ds(pl.multiple_of(k * vectors + x * block, block), block)
        at_near = pl.ds(pl.multiple_of(k * vectors + (1 - x) * block, block), block)
        for part in range(2):
            lanes = slice(part * vectors, (part + 1) * vectors)
            panel[at_mine, lanes] = mine[k][0, part]
            panel[at_near, lanes] = near[k][0, part]

    contract = (((1,), (1,)), ((), ()))
    right = lax.dot_general(left[src], panel[...], contract, preferred_element_type=F32).astype(BF16)

    @pl.when(pair > 0)
    def _():
        for k in range(count):
            store(k, pair - 1).wait()

    for m in range(moms):
        part = right[2 * m * columns : 2 * (m + 1) * columns]
        rows = jnp.concatenate([part[:, k * vectors : (k + 1) * vectors] for k in range(count)], 0)
        both = lax.dot_general(rows, sink[snk, m], contract, preferred_element_type=F32)
        for k in range(count):
            re = both[2 * k * columns : (2 * k + 1) * columns]
            im = both[(2 * k + 1) * columns : (2 * k + 2) * columns]
            done[k, m, 0] = (re[:, :vectors] - im[:, vectors:]).astype(BF16)
            done[k, m, 1] = (re[:, vectors:] + im[:, :vectors]).astype(BF16)
    for k in range(count):
        store(k, pair).start()

    @pl.when(pair == last)
    def _():
        for k in range(count):
            store(k, pair).wait()


def dress(out, out_shape, first_pair, pairs, dists, mine, near, left, sink, place, other_src, other_snk):
    _, _, block, vectors = mine[0][0].shape
    count = len(mine)
    moms = sink.shape[1]
    columns = out_shape.shape[3]
    whole = pl.BlockSpec(memory_space=pltpu.VMEM)
    chunks = [
        pl.BlockSpec((1, 2, block, vectors), lambda p, *_, first=first: (p + first, 0, 0, 0))
        for _, first in (*mine, *near)
    ]
    chained = out is not None
    operands = [left, sink, *(part for part, _ in (*mine, *near))] + ([out] if chained else [])
    in_specs = [whole, whole] + chunks + [pl.BlockSpec(memory_space=pl.ANY)] * chained
    macs = pairs * count * 2 * (2 * moms * columns) * (2 * vectors) * vectors
    return pl.pallas_call(
        functools.partial(dress_kernel, dists, chained, first_pair),
        out_shape=out_shape,
        grid_spec=pltpu.PrefetchScalarGridSpec(
            num_scalar_prefetch=3,
            grid=(pairs,),
            in_specs=in_specs,
            out_specs=pl.BlockSpec(memory_space=pl.ANY),
            scratch_shapes=[
                pltpu.VMEM((count * 2 * block, 2 * vectors), BF16),
                pltpu.VMEM((count, moms, 2, columns, vectors), BF16),
                pltpu.SemaphoreType.DMA((count,)),
            ],
        ),
        input_output_aliases={3 + len(operands) - 1: 0} if chained else {},
        compiler_params=params(1),
        cost_estimate=cost(2 * macs, 2**21),
        name="dress",
    )(place, other_src[first_pair : first_pair + pairs], other_snk[first_pair : first_pair + pairs], *operands)


CHUNKS = (1, 2, 2, 2)
HOOKS = [[], [('z', 3, 0)], [], [('x', 0, 0)], [('x', 3, 0), ('z', 1, 0)], [('z', 3, 1), ('x', 1, 0)], [('z', 2, 0), ('x', 3, 1), ('z', 1, 1)]]
LOCK = (False, False)
CALLS = ((0, 2, (0, 1, 2, 3)), (2, 2, (0, 1, 2, 3)))
GATES = {}
AFTER = {('x', 2, 1): [('x', 1, 1)]}
FROM = {('z', 2, 1): 4}


def exchange(value, axis, mask, among=lambda i: True):
    return lax.ppermute(value, axis, [(i, i ^ mask) for i in range(lax.axis_size(axis)) if among(i)])


def fast(eigvecs, momenta, pair_list, panels):
    vectors = eigvecs.shape[4]
    pair_count, _, rows, width = panels.shape
    moms = momenta.shape[0]
    space_count = lax.axis_size("space")
    spins = width // vectors
    space = lax.axis_index("space")
    tm = lax.axis_index("tm")
    x, z = space & 1, space >> 1
    low, high = z & 1, z >> 1
    where = [space, x, z, low, high, x * 4 + low * 2 + high, low * 4 + x * 2 + high]
    place = jnp.stack([value.astype(jnp.int32) for value in (*where, *momenta.reshape(-1))])
    other = (pair_list != tm).astype(jnp.int32)
    other_src, other_snk = other[:, 0], other[:, 1]

    factor = 1.0 / math.sqrt(6.0 * eigvecs.shape[3] * space_count * vectors)
    plan = [
        (d, c * (pair_count // n), pair_count // n) for d, n in enumerate(CHUNKS) for c in range(n)
    ]
    send_a, send_b, keep_a, keep_b = gram_halves(eigvecs[0], moms, place, factor)
    blocks = cut_panels(panels, vectors, plan, CUT_VMEM, place)

    raw, held, steps = {}, {}, []

    def fetch(name):
        if name not in raw:
            hop, d, c = name
            value = blocks[d, c] if hop == "z" or d == 0 else fetch(("z", d, c))
            if name in FROM:
                value, _ = lax.optimization_barrier((value, steps[FROM[name]]))
            raw[name] = exchange(meet(value, AFTER.get(name)), "space", 2 * d if hop == "z" else 1)
        held.setdefault(name, raw[name])
        return raw[name]

    def meet(value, names):
        if not names:
            return value
        for name in names:
            fetch(name)
        value, *came = lax.optimization_barrier((value, *(held[name] for name in names)))
        held.update(zip(names, came))
        return value

    along_x, low_z, high_z = 1, 2, 4

    def step(*sends):
        came = [exchange(value, "space", mask) for value, mask in sends]
        came[0] = meet(came[0], HOOKS[len(steps)])
        steps.append(came[0])
        return came

    came = step((send_a, along_x), (send_b, low_z))
    send_a, send_b, keep_a, keep_b = fold(fold_kernel, keep_a, keep_b, *came, place)
    came = step((send_a, low_z), (send_b, along_x))
    send, keep = fold(join_kernel, keep_a, keep_b, *came, place)
    (came,) = step((send, high_z))
    field = (keep + came.astype(F32)).astype(BF16)[None]
    (came,) = step((field, high_z))
    own, oth = [], []

    def share(both):
        own.append(both)
        oth.append(exchange(both, "tm", 1))

    def after_share(value, count):
        if len(oth) >= count:
            value, oth[count - 1] = lax.optimization_barrier((value, oth[count - 1]))
        return value

    *parts, both = gather(halve_kernel, field, came)
    share(both)
    came = step((parts[0], low_z), (parts[1], along_x))
    if LOCK[0]:
        came[0] = after_share(came[0], 1)
    *parts, both = gather(pair_kernel, *parts, *came)
    share(both)
    came = step((parts[0], along_x), (parts[1], low_z))
    if LOCK[1]:
        came[0] = after_share(came[0], 2)
    share(*gather(both_kernel, *came))
    oth[2] = meet(oth[2], HOOKS[6])

    columns = width // space_count
    out_shape = jax.ShapeDtypeStruct((pair_count, moms, 2, columns, width), BF16)

    def part(hop, d, first):
        c, at = divmod(first, pair_count // CHUNKS[d])
        if (hop, d) == ("z", 0):
            return blocks[0, c], at
        fetch((hop, d, c))
        return held[hop, d, c], at

    left, sink = prepare(own, oth, columns, place)
    out = None
    for call, (first, pairs, dists) in enumerate(CALLS):
        for _, d, c in GATES.get(call, ()):
            value, out = lax.optimization_barrier((fetch(("z", d, c)), out))
            raw["z", d, c] = held["z", d, c] = value
        mine = [part("z", d, first) for d in dists]
        near = [part("x", d, first) for d in dists]
        out = dress(
            out, out_shape, first, pairs, dists, mine, near, left, sink, place, other_src, other_snk
        )
    return out


def phased_block(cosine, sine_part, real_part, imag_part):
    cos_col = cosine[:, None]
    sin_col = sine_part[:, None]
    wave_re = cos_col * real_part + sin_col * imag_part
    wave_im = cos_col * imag_part - sin_col * real_part
    upper = jnp.concatenate([wave_re, wave_im], -1)
    lower = jnp.concatenate([wave_im, -wave_re], -1)
    return jnp.stack([upper, lower], -4).astype(jnp.bfloat16)


def general(eigvecs, momenta, pair_list, panels):
    slice_count, _, colors, slab_sites, vectors = eigvecs.shape
    mom_count = momenta.shape[0]
    space_count = lax.axis_size("space")
    first_site = lax.axis_index("space") * slab_sites
    site_index = first_site + jnp.arange(slab_sites, dtype=jnp.int32)
    xpos = site_index % LX
    ypos = site_index // LX % LX
    zpos = site_index // (LX * LX)
    wave = (
        momenta[:, 0:1] * xpos[None, :]
        + momenta[:, 1:2] * ypos[None, :]
        + momenta[:, 2:3] * zpos[None, :]
    )
    wave = jnp.mod(wave, LX)
    angle = wave.astype(jnp.float32) * jnp.float32(2.0 * math.pi / LX)
    cosine = jnp.cos(angle)
    sine_part = jnp.sin(angle)
    factor = 1.0 / math.sqrt(6.0 * slab_sites * space_count * vectors)
    real_part = eigvecs[:, 0].astype(jnp.float32)
    imag_part = eigvecs[:, 1].astype(jnp.float32)
    phased_all = jnp.concatenate(
        [
            phased_block(cosine[moment], sine_part[moment], real_part, imag_part)
            for moment in range(mom_count)
        ],
        -1,
    )
    phased_all = phased_all.reshape(slice_count, 2, colors, slab_sites, mom_count, 2 * vectors)
    gram_local = jnp.einsum(
        "trcsk,trcsml->tmkl", eigvecs, phased_all, preferred_element_type=jnp.float32
    )
    gram_local = factor * gram_local
    summed = lax.psum(gram_local, "space")
    own_fields = summed.astype(jnp.bfloat16)
    meson_fields = lax.all_gather(own_fields, "tm", axis=0, tiled=True)
    pair_count = pair_list.shape[0]
    panel_rows = panels.shape[2]
    panel_width = panels.shape[3]
    spins = panel_width // vectors
    source_fields = jnp.take(meson_fields, pair_list[:, 0], axis=0).reshape(
        pair_count, mom_count, vectors, 2, vectors
    )
    sink_fields = jnp.take(meson_fields, pair_list[:, 1], axis=0).reshape(
        pair_count, mom_count, vectors, 2, vectors
    )
    panel_parts = panels.reshape(pair_count, 2, panel_rows, spins, vectors)
    panel_re = panel_parts[:, 0]
    panel_im = panel_parts[:, 1]
    panel_mix = jnp.stack(
        [jnp.stack([panel_re, panel_im], 1), jnp.stack([panel_im, -panel_re], 1)], 1
    )
    right_dressed = jnp.einsum(
        "porxbk,pmlrk->pmoxbl", panel_mix, source_fields, preferred_element_type=jnp.float32
    )
    right_dressed = right_dressed.astype(jnp.bfloat16).reshape(
        pair_count * mom_count, 2, panel_rows, panel_width
    )
    turned = lax.all_to_all(right_dressed, "space", split_axis=3, concat_axis=2, tiled=True)
    column_count = turned.shape[3]
    turned = turned.reshape(pair_count, mom_count, 2, spins, vectors, column_count)
    turned_re = turned[:, :, 0]
    turned_im = turned[:, :, 1]
    mixed_parts = jnp.stack(
        [jnp.stack([turned_re, -turned_im], 2), jnp.stack([turned_im, turned_re], 2)], 2
    )
    dressed = jnp.einsum(
        "pmorajc,pmkrj->pmocak", mixed_parts, sink_fields, preferred_element_type=jnp.float32
    )
    return dressed.reshape(pair_count, mom_count, 2, column_count, panel_width).astype(jnp.bfloat16)


def local(eigvecs, momenta, pair_list, panels):
    slices, _, _, sites, vectors = eigvecs.shape
    pairs, _, rows, width = panels.shape
    space_count = lax.axis_size("space")
    spins = width // vectors
    fits = (
        slices == 1
        and lax.axis_size("tm") == 2
        and space_count == 2 * spins
        and spins == 4
        and rows * space_count == width
        and rows % 128 == 0
        and (vectors // space_count) % 16 == 0
        and sites % 16 == 0
        and pairs % 2 == 0
        and momenta.shape[0] <= 8
    )
    return (fast if fits else general)(eigvecs, momenta, pair_list, panels)


def solution(mesh):
    placed = (
        P(("cfg", "tm"), None, None, "space", None),
        P(),
        P("tm", None),
        P(("cfg", "tm"), None, "space", None),
    )
    return jax.shard_map(
        local,
        mesh=mesh,
        in_specs=placed,
        out_specs=P(("cfg", "tm"), None, None, "space", None),
        check_vma=False,
    )
```

```python
import functools
import math

import jax
import jax.numpy as jnp
from jax import lax
from jax.experimental import pallas as pl
from jax.experimental.pallas import tpu as pltpu
from jax.sharding import PartitionSpec as P

LX = 64
LX_BITS = LX.bit_length() - 1
F32, BF16 = jnp.float32, jnp.bfloat16
SPACE, X, Z, Z_LOW, Z_HIGH, HERE_A, HERE_B, MOMENTA = range(8)
VMEM_LIMIT = 24 * 1024 * 1024
CUT_VMEM = 24 * 1024 * 1024


def params(steps=0):
    return pltpu.CompilerParams(
        vmem_limit_bytes=VMEM_LIMIT, dimension_semantics=("arbitrary",) * steps or None
    )


def cost(flops, bytes_accessed):
    return pl.CostEstimate(flops=int(flops), bytes_accessed=int(bytes_accessed), transcendentals=0)


def gram_kernel(factor, place, eig, send_a, send_b, keep_a, keep_b, phased, total):
    colors, sites, vectors = eig.shape[1:]
    moms, half = send_a.shape[:2]
    site = place[SPACE] * sites + lax.broadcasted_iota(jnp.int32, (sites, 128), 0)
    lane = lax.broadcasted_iota(jnp.int32, (sites, 128), 1)
    coords = (site & (LX - 1), (site >> LX_BITS) & (LX - 1), site >> (2 * LX_BITS))
    wave = jnp.zeros((sites, 128), jnp.int32)
    for m in range(moms):
        mine = sum(place[MOMENTA + 3 * m + j] * coords[j] for j in range(3))
        wave = jnp.where(lane == m, mine, wave)
    angle = (wave & (LX - 1)).astype(F32) * F32(2.0 * math.pi / LX)
    cosine, sine = jnp.cos(angle), jnp.sin(angle)
    rows = colors * sites
    both = eig[...].reshape(2 * rows, vectors)
    for m in range(moms):
        c, s = cosine[:, m : m + 1], sine[:, m : m + 1]
        for color in range(colors):
            re, im = eig[0, color].astype(F32), eig[1, color].astype(F32)
            wave_re, wave_im = c * re + s * im, c * im - s * re
            at = color * sites
            phased[at : at + sites, :vectors] = wave_re.astype(BF16)
            phased[at : at + sites, vectors:] = wave_im.astype(BF16)
            at += rows
            phased[at : at + sites, :vectors] = wave_im.astype(BF16)
            phased[at : at + sites, vectors:] = (-wave_re).astype(BF16)
        total[...] = factor * lax.dot_general(
            both, phased[...], (((0,), (0,)), ((), ())), preferred_element_type=F32
        )
        for send, keep, bit, lanes in (
            (send_a, keep_a, place[X], slice(None, vectors)),
            (send_b, keep_b, place[Z_LOW], slice(vectors, None)),
        ):
            send[m] = total[pl.ds(pl.multiple_of((1 - bit) * half, half), half), lanes].astype(BF16)
            keep[m] = total[pl.ds(pl.multiple_of(bit * half, half), half), lanes]


def gram_halves(eig, moms, place, factor):
    _, colors, sites, vectors = eig.shape
    shape = (moms, vectors // 2, vectors)
    smem = pl.BlockSpec(memory_space=pltpu.SMEM)
    vmem = pl.BlockSpec(memory_space=pltpu.VMEM)
    return pl.pallas_call(
        functools.partial(gram_kernel, factor),
        out_shape=[jax.ShapeDtypeStruct(shape, kind) for kind in (BF16, BF16, F32, F32)],
        in_specs=[smem, vmem],
        out_specs=[vmem] * 4,
        scratch_shapes=[
            pltpu.VMEM((2 * colors * sites, 2 * vectors), BF16),
            pltpu.VMEM((vectors, 2 * vectors), F32),
        ],
        compiler_params=params(),
        cost_estimate=cost(4 * colors * sites * vectors * moms * 2 * vectors, 3 * 2**20),
        name="gram",
    )(place, eig)


def cut_kernel(plan, place, panels, *refs):
    cuts, sems = refs[:-1], refs[-1]
    vectors = cuts[0].shape[3]
    copies = []
    for i, (d, first, _) in enumerate(plan):
        lanes = pl.ds(pl.multiple_of((place[Z] ^ d) * vectors, vectors), vectors)
        source = panels.at[first : first + cuts[i].shape[0], :, :, lanes]
        copies.append(pltpu.make_async_copy(source, cuts[i], sems.at[i]))
        copies[-1].start()
    for copy in copies:
        copy.wait()


def cut_panels(panels, vectors, plan, vmem, place):
    cuts = pl.pallas_call(
        functools.partial(cut_kernel, plan),
        out_shape=[jax.ShapeDtypeStruct((size, *panels.shape[1:3], vectors), BF16) for _, _, size in plan],
        in_specs=[pl.BlockSpec(memory_space=pltpu.SMEM), pl.BlockSpec(memory_space=pl.ANY)],
        out_specs=[pl.BlockSpec(memory_space=pltpu.VMEM)] * len(plan),
        scratch_shapes=[pltpu.SemaphoreType.DMA((len(plan),))],
        compiler_params=pltpu.CompilerParams(vmem_limit_bytes=vmem),
        cost_estimate=cost(0, 4 * panels.size),
        name="cut",
    )(place, panels)
    return {(d, first // size): cut for (d, first, size), cut in zip(plan, cuts)}


def fold_kernel(place, keep_a, keep_b, came_a, came_b, send_a, send_b, left_a, left_b):
    half = send_a.shape[1]
    for keep, came, bit, send, left in (
        (keep_a, came_a, place[Z_LOW], send_a, left_a),
        (keep_b, came_b, place[X], send_b, left_b),
    ):
        own = pl.ds(pl.multiple_of(bit * half, half), half)
        off = pl.ds(pl.multiple_of((1 - bit) * half, half), half)
        left[...] = keep[:, own, :] + came[:, own, :].astype(F32)
        send[...] = (keep[:, off, :] + came[:, off, :].astype(F32)).astype(BF16)


def join_kernel(place, keep_a, keep_b, came_a, came_b, send, left):
    half, width = send.shape[1:]
    bit = place[Z_HIGH]
    own = pl.ds(pl.multiple_of(bit * half, half), half)
    off = pl.ds(pl.multiple_of((1 - bit) * half, half), half)
    for keep, came, lanes in (
        (keep_a, came_a, slice(None, width // 2)),
        (keep_b, came_b, slice(width // 2, None)),
    ):
        left[:, :, lanes] = keep[:, own, :] + came[:, own, :].astype(F32)
        send[:, :, lanes] = (keep[:, off, :] + came[:, off, :].astype(F32)).astype(BF16)


def fold(kernel, keep_a, keep_b, came_a, came_b, place):
    moms, rows, width = keep_a.shape
    if kernel is join_kernel:
        shape, kinds = (moms, rows // 2, 2 * width), (BF16, F32)
    else:
        shape, kinds = (moms, rows // 2, width), (BF16, BF16, F32, F32)
    vmem = pl.BlockSpec(memory_space=pltpu.VMEM)
    return pl.pallas_call(
        kernel,
        out_shape=[jax.ShapeDtypeStruct(shape, kind) for kind in kinds],
        in_specs=[pl.BlockSpec(memory_space=pltpu.SMEM)] + [vmem] * 4,
        out_specs=[vmem] * len(kinds),
        compiler_params=params(),
        cost_estimate=cost(2 * keep_a.size, 16 * keep_a.size),
        name="fold",
    )(place, keep_a, keep_b, came_a, came_b)


def halve_kernel(field, came, part_a, part_b, both):
    vectors = part_a.shape[3]
    for i, piece in enumerate((field, came)):
        for j, part in enumerate((part_a, part_b)):
            value = piece[0, :, :, j * vectors : (j + 1) * vectors]
            part[i] = value
            both[j, i] = value


def pair_kernel(own_a, own_b, came_a, came_b, part_a, part_b, both):
    count = own_a.shape[0]
    for j, (own, came, part) in enumerate(((own_a, came_a, part_a), (own_b, came_b, part_b))):
        part[:count] = own[...]
        part[count:] = came[...]
        both[j] = came[...]


def both_kernel(came_a, came_b, both):
    both[0] = came_a[...]
    both[1] = came_b[...]


def gather(kernel, *pieces):
    count, moms, rows, width = pieces[0].shape
    shapes = {
        halve_kernel: [(2 * count, moms, rows, width // 2)] * 2 + [(2, 2 * count, moms, rows, width // 2)],
        pair_kernel: [(2 * count, moms, rows, width)] * 2 + [(2, count, moms, rows, width)],
        both_kernel: [(2, count, moms, rows, width)],
    }[kernel]
    vmem = pl.BlockSpec(memory_space=pltpu.VMEM)
    return pl.pallas_call(
        kernel,
        out_shape=[jax.ShapeDtypeStruct(shape, BF16) for shape in shapes],
        in_specs=[vmem] * len(pieces),
        out_specs=[vmem] * len(shapes),
        compiler_params=params(),
        cost_estimate=cost(0, 4 * len(pieces) * pieces[0].size),
        name="gather",
    )(*pieces)


def prepare_kernel(groups, place, *refs):
    fields, (left, sink) = refs[:-2], refs[-2:]
    moms, piece_rows, vectors = fields[0].shape[2:]
    columns = left.shape[1] // (2 * moms)
    per = columns // piece_rows
    x = place[X]
    for t in range(2):
        for p, here in enumerate((place[HERE_A], place[HERE_B])):
            j = 0
            for field in fields[t * groups : (t + 1) * groups]:
                for i in range(field.shape[1]):
                    q = here ^ j
                    j += 1
                    to_sink = pl.ds(pl.multiple_of(p * vectors + q * piece_rows, piece_rows), piece_rows)
                    for m in range(moms):
                        sink[t, m, to_sink] = field[p, i, m]

                    @pl.when(q // per == x)
                    def _(field=field, i=i, q=q):
                        for m in range(moms):
                            rows = field[p, i, m]
                            at = pl.multiple_of(2 * m * columns + (q - x * per) * piece_rows, piece_rows)
                            up, down = pl.ds(at, piece_rows), pl.ds(at + columns, piece_rows)
                            if p == 0:
                                left[t, up, :vectors] = rows
                                left[t, down, vectors:] = rows
                            else:
                                left[t, up, vectors:] = rows
                                left[t, down, :vectors] = -rows


def prepare(own, oth, columns, place):
    moms, piece_rows, vectors = own[0].shape[2:]
    vmem = pl.BlockSpec(memory_space=pltpu.VMEM)
    return pl.pallas_call(
        functools.partial(prepare_kernel, len(own)),
        out_shape=(
            jax.ShapeDtypeStruct((2, 2 * moms * columns, 2 * vectors), BF16),
            jax.ShapeDtypeStruct((2, moms, 2 * vectors, vectors), BF16),
        ),
        in_specs=[pl.BlockSpec(memory_space=pltpu.SMEM)] + [vmem] * (len(own) + len(oth)),
        out_specs=(vmem, vmem),
        compiler_params=params(),
        cost_estimate=cost(0, 16 * own[-1].size),
        name="prepare",
    )(place, *own, *oth)


def dress_kernel(count, chained, place, other_src, other_snk, left, sink, *refs):
    mine, near = refs[:count], refs[count : 2 * count]
    out, panel = refs[2 * count + chained :]
    moms, width, vectors = sink.shape[1:]
    columns = out.shape[3]
    pair = pl.program_id(0)
    x, z = place[X], place[Z]
    src, snk = other_src[pair], other_snk[pair]
    block = mine[0].shape[2]
    for k in range(count):
        base = (z ^ k) * vectors
        at_mine = pl.ds(pl.multiple_of(base + x * block, block), block)
        at_near = pl.ds(pl.multiple_of(base + (1 - x) * block, block), block)
        for part in range(2):
            lanes = slice(part * vectors, (part + 1) * vectors)
            panel[at_mine, lanes] = mine[k][0, part]
            panel[at_near, lanes] = near[k][0, part]

    contract = (((1,), (1,)), ((), ()))
    right = lax.dot_general(left[src], panel[...], contract, preferred_element_type=F32).astype(BF16)
    for m in range(moms):
        part = right[2 * m * columns : 2 * (m + 1) * columns]
        rows = jnp.concatenate([part[:, k * vectors : (k + 1) * vectors] for k in range(count)], 0)
        both = lax.dot_general(rows, sink[snk, m], contract, preferred_element_type=F32)
        for k in range(count):
            at = slice(k * vectors, (k + 1) * vectors)
            re = both[2 * k * columns : (2 * k + 1) * columns]
            im = both[(2 * k + 1) * columns : (2 * k + 2) * columns]
            out[0, m, 0, :, at] = (re[:, :vectors] - im[:, vectors:]).astype(BF16)
            out[0, m, 1, :, at] = (re[:, vectors:] + im[:, :vectors]).astype(BF16)


def dress(out, out_shape, first_pair, pairs, mine, near, left, sink, place, other_src, other_snk):
    _, _, block, vectors = mine[0][0].shape
    count = len(mine)
    moms = sink.shape[1]
    columns = out_shape.shape[3]
    whole = pl.BlockSpec(memory_space=pltpu.VMEM)
    chunks = [
        pl.BlockSpec((1, 2, block, vectors), lambda p, *_, first=first: (p + first, 0, 0, 0))
        for _, first in (*mine, *near)
    ]
    chained = out is not None
    operands = [left, sink, *(part for part, _ in (*mine, *near))] + ([out] if chained else [])
    in_specs = [whole, whole] + chunks + [pl.BlockSpec(memory_space=pl.ANY)] * chained
    macs = pairs * count * 2 * (2 * moms * columns) * (2 * vectors) * vectors
    return pl.pallas_call(
        functools.partial(dress_kernel, count, chained),
        out_shape=out_shape,
        grid_spec=pltpu.PrefetchScalarGridSpec(
            num_scalar_prefetch=3,
            grid=(pairs,),
            in_specs=in_specs,
            out_specs=pl.BlockSpec(
                (1, moms, 2, columns, count * vectors), lambda p, *_: (p + first_pair, 0, 0, 0, 0)
            ),
            scratch_shapes=[pltpu.VMEM((count * 2 * block, 2 * vectors), BF16)],
        ),
        input_output_aliases={3 + len(operands) - 1: 0} if chained else {},
        compiler_params=params(1),
        cost_estimate=cost(2 * macs, 2**21),
        name="dress",
    )(place, other_src[first_pair : first_pair + pairs], other_snk[first_pair : first_pair + pairs], *operands)


CHUNKS = (1, 2, 2, 2)
HOOKS = [
    [],
    [("z", 3, 0)],
    [],
    [("x", 0, 0), ("z", 1, 0)],
    [("x", 3, 0)],
    [("z", 3, 1), ("x", 1, 0)],
    [("z", 2, 0), ("x", 3, 1), ("z", 1, 1)],
]
CALLS = ((0, 2), (2, 2))
AFTER = {("x", 2, 1): [("x", 1, 1)]}
FROM = {("z", 2, 1): 4}


def exchange(value, axis, mask, among=lambda i: True):
    return lax.ppermute(value, axis, [(i, i ^ mask) for i in range(lax.axis_size(axis)) if among(i)])


def fast(eigvecs, momenta, pair_list, panels):
    vectors = eigvecs.shape[4]
    pair_count, _, rows, width = panels.shape
    moms = momenta.shape[0]
    space_count = lax.axis_size("space")
    spins = width // vectors
    space = lax.axis_index("space")
    tm = lax.axis_index("tm")
    x, z = space & 1, space >> 1
    low, high = z & 1, z >> 1
    where = [space, x, z, low, high, x * 4 + low * 2 + high, low * 4 + x * 2 + high]
    place = jnp.stack([value.astype(jnp.int32) for value in (*where, *momenta.reshape(-1))])
    other = (pair_list != tm).astype(jnp.int32)
    other_src, other_snk = other[:, 0], other[:, 1]

    factor = 1.0 / math.sqrt(6.0 * eigvecs.shape[3] * space_count * vectors)
    plan = [
        (d, c * (pair_count // n), pair_count // n) for d, n in enumerate(CHUNKS) for c in range(n)
    ]
    send_a, send_b, keep_a, keep_b = gram_halves(eigvecs[0], moms, place, factor)
    blocks = cut_panels(panels, vectors, plan, CUT_VMEM, place)

    raw, held, steps = {}, {}, []

    def fetch(name):
        if name not in raw:
            hop, d, c = name
            value = blocks[d, c] if hop == "z" or d == 0 else fetch(("z", d, c))
            if name in FROM:
                value, _ = lax.optimization_barrier((value, steps[FROM[name]]))
            raw[name] = exchange(meet(value, AFTER.get(name)), "space", 2 * d if hop == "z" else 1)
        held.setdefault(name, raw[name])
        return raw[name]

    def meet(value, names):
        if not names:
            return value
        for name in names:
            fetch(name)
        value, *came = lax.optimization_barrier((value, *(held[name] for name in names)))
        held.update(zip(names, came))
        return value

    along_x, low_z, high_z = 1, 2, 4

    def step(*sends):
        came = [exchange(value, "space", mask) for value, mask in sends]
        came[0] = meet(came[0], HOOKS[len(steps)])
        steps.append(came[0])
        return came

    came = step((send_a, along_x), (send_b, low_z))
    send_a, send_b, keep_a, keep_b = fold(fold_kernel, keep_a, keep_b, *came, place)
    came = step((send_a, low_z), (send_b, along_x))
    send, keep = fold(join_kernel, keep_a, keep_b, *came, place)
    (came,) = step((send, high_z))
    field = (keep + came.astype(F32)).astype(BF16)[None]
    (came,) = step((field, high_z))
    own, oth = [], []

    def share(both):
        own.append(both)
        oth.append(exchange(both, "tm", 1))

    *parts, both = gather(halve_kernel, field, came)
    share(both)
    came = step((parts[0], low_z), (parts[1], along_x))
    *parts, both = gather(pair_kernel, *parts, *came)
    share(both)
    came = step((parts[0], along_x), (parts[1], low_z))
    share(*gather(both_kernel, *came))
    oth[2] = meet(oth[2], HOOKS[6])

    columns = width // space_count
    out_shape = jax.ShapeDtypeStruct((pair_count, moms, 2, columns, width), BF16)

    def part(hop, d, first):
        c, at = divmod(first, pair_count // CHUNKS[d])
        if (hop, d) == ("z", 0):
            return blocks[0, c], at
        fetch((hop, d, c))
        return held[hop, d, c], at

    left, sink = prepare(own, oth, columns, place)
    out = None
    dists = range(spins)
    for first, pairs in CALLS:
        mine = [part("z", d, first) for d in dists]
        near = [part("x", d, first) for d in dists]
        out = dress(
            out, out_shape, first, pairs, mine, near, left, sink, place, other_src, other_snk
        )
    return out


def phased_block(cosine, sine_part, real_part, imag_part):
    cos_col = cosine[:, None]
    sin_col = sine_part[:, None]
    wave_re = cos_col * real_part + sin_col * imag_part
    wave_im = cos_col * imag_part - sin_col * real_part
    upper = jnp.concatenate([wave_re, wave_im], -1)
    lower = jnp.concatenate([wave_im, -wave_re], -1)
    return jnp.stack([upper, lower], -4).astype(jnp.bfloat16)


def general(eigvecs, momenta, pair_list, panels):
    slice_count, _, colors, slab_sites, vectors = eigvecs.shape
    mom_count = momenta.shape[0]
    space_count = lax.axis_size("space")
    first_site = lax.axis_index("space") * slab_sites
    site_index = first_site + jnp.arange(slab_sites, dtype=jnp.int32)
    xpos = site_index % LX
    ypos = site_index // LX % LX
    zpos = site_index // (LX * LX)
    wave = (
        momenta[:, 0:1] * xpos[None, :]
        + momenta[:, 1:2] * ypos[None, :]
        + momenta[:, 2:3] * zpos[None, :]
    )
    wave = jnp.mod(wave, LX)
    angle = wave.astype(jnp.float32) * jnp.float32(2.0 * math.pi / LX)
    cosine = jnp.cos(angle)
    sine_part = jnp.sin(angle)
    factor = 1.0 / math.sqrt(6.0 * slab_sites * space_count * vectors)
    real_part = eigvecs[:, 0].astype(jnp.float32)
    imag_part = eigvecs[:, 1].astype(jnp.float32)
    phased_all = jnp.concatenate(
        [
            phased_block(cosine[moment], sine_part[moment], real_part, imag_part)
            for moment in range(mom_count)
        ],
        -1,
    )
    phased_all = phased_all.reshape(slice_count, 2, colors, slab_sites, mom_count, 2 * vectors)
    gram_local = jnp.einsum(
        "trcsk,trcsml->tmkl", eigvecs, phased_all, preferred_element_type=jnp.float32
    )
    gram_local = factor * gram_local
    summed = lax.psum(gram_local, "space")
    own_fields = summed.astype(jnp.bfloat16)
    meson_fields = lax.all_gather(own_fields, "tm", axis=0, tiled=True)
    pair_count = pair_list.shape[0]
    panel_rows = panels.shape[2]
    panel_width = panels.shape[3]
    spins = panel_width // vectors
    source_fields = jnp.take(meson_fields, pair_list[:, 0], axis=0).reshape(
        pair_count, mom_count, vectors, 2, vectors
    )
    sink_fields = jnp.take(meson_fields, pair_list[:, 1], axis=0).reshape(
        pair_count, mom_count, vectors, 2, vectors
    )
    panel_parts = panels.reshape(pair_count, 2, panel_rows, spins, vectors)
    panel_re = panel_parts[:, 0]
    panel_im = panel_parts[:, 1]
    panel_mix = jnp.stack(
        [jnp.stack([panel_re, panel_im], 1), jnp.stack([panel_im, -panel_re], 1)], 1
    )
    right_dressed = jnp.einsum(
        "porxbk,pmlrk->pmoxbl", panel_mix, source_fields, preferred_element_type=jnp.float32
    )
    right_dressed = right_dressed.astype(jnp.bfloat16).reshape(
        pair_count * mom_count, 2, panel_rows, panel_width
    )
    turned = lax.all_to_all(right_dressed, "space", split_axis=3, concat_axis=2, tiled=True)
    column_count = turned.shape[3]
    turned = turned.reshape(pair_count, mom_count, 2, spins, vectors, column_count)
    turned_re = turned[:, :, 0]
    turned_im = turned[:, :, 1]
    mixed_parts = jnp.stack(
        [jnp.stack([turned_re, -turned_im], 2), jnp.stack([turned_im, turned_re], 2)], 2
    )
    dressed = jnp.einsum(
        "pmorajc,pmkrj->pmocak", mixed_parts, sink_fields, preferred_element_type=jnp.float32
    )
    return dressed.reshape(pair_count, mom_count, 2, column_count, panel_width).astype(jnp.bfloat16)


def local(eigvecs, momenta, pair_list, panels):
    slices, _, _, sites, vectors = eigvecs.shape
    pairs, _, rows, width = panels.shape
    space_count = lax.axis_size("space")
    spins = width // vectors
    fits = (
        slices == 1
        and lax.axis_size("tm") == 2
        and space_count == 2 * spins
        and spins == 4
        and rows * space_count == width
        and rows % 128 == 0
        and (vectors // space_count) % 16 == 0
        and sites % 16 == 0
        and pairs % 2 == 0
        and momenta.shape[0] <= 8
    )
    return (fast if fits else general)(eigvecs, momenta, pair_list, panels)


def solution(mesh):
    placed = (
        P(("cfg", "tm"), None, None, "space", None),
        P(),
        P("tm", None),
        P(("cfg", "tm"), None, "space", None),
    )
    return jax.shard_map(
        local,
        mesh=mesh,
        in_specs=placed,
        out_specs=P(("cfg", "tm"), None, None, "space", None),
        check_vma=False,
    )
```

```python
import functools
import math

import jax
import jax.numpy as jnp
from jax import lax
from jax.experimental import pallas as pl
from jax.experimental.pallas import tpu as pltpu
from jax.sharding import PartitionSpec as P

LX = 64
LX_BITS = LX.bit_length() - 1
F32, BF16 = jnp.float32, jnp.bfloat16
SPACE, X, Z, Z_LOW, Z_HIGH, HERE_A, HERE_B, MOMENTA = range(8)
VMEM_LIMIT = 24 * 1024 * 1024
CUT_VMEM = 24 * 1024 * 1024


def params(steps=0):
    return pltpu.CompilerParams(
        vmem_limit_bytes=VMEM_LIMIT, dimension_semantics=("arbitrary",) * steps or None
    )


def cost(flops, bytes_accessed):
    return pl.CostEstimate(flops=int(flops), bytes_accessed=int(bytes_accessed), transcendentals=0)


def gram_kernel(factor, place, eig, send_a, send_b, keep_a, keep_b, phased, total):
    colors, sites, vectors = eig.shape[1:]
    moms, half = send_a.shape[:2]
    site = place[SPACE] * sites + lax.broadcasted_iota(jnp.int32, (sites, 128), 0)
    lane = lax.broadcasted_iota(jnp.int32, (sites, 128), 1)
    coords = (site & (LX - 1), (site >> LX_BITS) & (LX - 1), site >> (2 * LX_BITS))
    wave = jnp.zeros((sites, 128), jnp.int32)
    for m in range(moms):
        mine = sum(place[MOMENTA + 3 * m + j] * coords[j] for j in range(3))
        wave = jnp.where(lane == m, mine, wave)
    angle = (wave & (LX - 1)).astype(F32) * F32(2.0 * math.pi / LX)
    cosine, sine = jnp.cos(angle), jnp.sin(angle)
    rows = colors * sites
    both = eig[...].reshape(2 * rows, vectors)
    for m in range(moms):
        c, s = cosine[:, m : m + 1], sine[:, m : m + 1]
        for color in range(colors):
            re, im = eig[0, color].astype(F32), eig[1, color].astype(F32)
            wave_re, wave_im = c * re + s * im, c * im - s * re
            at = color * sites
            phased[at : at + sites, :vectors] = wave_re.astype(BF16)
            phased[at : at + sites, vectors:] = wave_im.astype(BF16)
            at += rows
            phased[at : at + sites, :vectors] = wave_im.astype(BF16)
            phased[at : at + sites, vectors:] = (-wave_re).astype(BF16)
        total[...] = factor * lax.dot_general(
            both, phased[...], (((0,), (0,)), ((), ())), preferred_element_type=F32
        )
        for send, keep, bit, lanes in (
            (send_a, keep_a, place[X], slice(None, vectors)),
            (send_b, keep_b, place[Z_LOW], slice(vectors, None)),
        ):
            send[m] = total[pl.ds(pl.multiple_of((1 - bit) * half, half), half), lanes].astype(BF16)
            keep[m] = total[pl.ds(pl.multiple_of(bit * half, half), half), lanes]


def gram_halves(eig, moms, place, factor):
    _, colors, sites, vectors = eig.shape
    shape = (moms, vectors // 2, vectors)
    smem = pl.BlockSpec(memory_space=pltpu.SMEM)
    vmem = pl.BlockSpec(memory_space=pltpu.VMEM)
    return pl.pallas_call(
        functools.partial(gram_kernel, factor),
        out_shape=[jax.ShapeDtypeStruct(shape, kind) for kind in (BF16, BF16, F32, F32)],
        in_specs=[smem, vmem],
        out_specs=[vmem] * 4,
        scratch_shapes=[
            pltpu.VMEM((2 * colors * sites, 2 * vectors), BF16),
            pltpu.VMEM((vectors, 2 * vectors), F32),
        ],
        compiler_params=params(),
        cost_estimate=cost(4 * colors * sites * vectors * moms * 2 * vectors, 3 * 2**20),
        name="gram",
    )(place, eig)


def cut_kernel(plan, place, panels, *refs):
    cuts, sems = refs[:-1], refs[-1]
    vectors = cuts[0].shape[3]
    copies = []
    for i, (d, first, _) in enumerate(plan):
        lanes = pl.ds(pl.multiple_of((place[Z] ^ d) * vectors, vectors), vectors)
        source = panels.at[first : first + cuts[i].shape[0], :, :, lanes]
        copies.append(pltpu.make_async_copy(source, cuts[i], sems.at[i]))
        copies[-1].start()
    for copy in copies:
        copy.wait()


def cut_panels(panels, vectors, plan, vmem, place):
    cuts = pl.pallas_call(
        functools.partial(cut_kernel, plan),
        out_shape=[jax.ShapeDtypeStruct((size, *panels.shape[1:3], vectors), BF16) for _, _, size in plan],
        in_specs=[pl.BlockSpec(memory_space=pltpu.SMEM), pl.BlockSpec(memory_space=pl.ANY)],
        out_specs=[pl.BlockSpec(memory_space=pltpu.VMEM)] * len(plan),
        scratch_shapes=[pltpu.SemaphoreType.DMA((len(plan),))],
        compiler_params=pltpu.CompilerParams(vmem_limit_bytes=vmem),
        cost_estimate=cost(0, 4 * panels.size),
        name="cut",
    )(place, panels)
    return {(d, first // size): cut for (d, first, size), cut in zip(plan, cuts)}


def fold_kernel(place, keep_a, keep_b, came_a, came_b, send_a, send_b, left_a, left_b):
    half = send_a.shape[1]
    for keep, came, bit, send, left in (
        (keep_a, came_a, place[Z_LOW], send_a, left_a),
        (keep_b, came_b, place[X], send_b, left_b),
    ):
        own = pl.ds(pl.multiple_of(bit * half, half), half)
        off = pl.ds(pl.multiple_of((1 - bit) * half, half), half)
        left[...] = keep[:, own, :] + came[:, own, :].astype(F32)
        send[...] = (keep[:, off, :] + came[:, off, :].astype(F32)).astype(BF16)


def join_kernel(place, keep_a, keep_b, came_a, came_b, send, left):
    half, width = send.shape[1:]
    bit = place[Z_HIGH]
    own = pl.ds(pl.multiple_of(bit * half, half), half)
    off = pl.ds(pl.multiple_of((1 - bit) * half, half), half)
    for keep, came, lanes in (
        (keep_a, came_a, slice(None, width // 2)),
        (keep_b, came_b, slice(width // 2, None)),
    ):
        left[:, :, lanes] = keep[:, own, :] + came[:, own, :].astype(F32)
        send[:, :, lanes] = (keep[:, off, :] + came[:, off, :].astype(F32)).astype(BF16)


def fold(kernel, keep_a, keep_b, came_a, came_b, place):
    moms, rows, width = keep_a.shape
    if kernel is join_kernel:
        shape, kinds = (moms, rows // 2, 2 * width), (BF16, F32)
    else:
        shape, kinds = (moms, rows // 2, width), (BF16, BF16, F32, F32)
    vmem = pl.BlockSpec(memory_space=pltpu.VMEM)
    return pl.pallas_call(
        kernel,
        out_shape=[jax.ShapeDtypeStruct(shape, kind) for kind in kinds],
        in_specs=[pl.BlockSpec(memory_space=pltpu.SMEM)] + [vmem] * 4,
        out_specs=[vmem] * len(kinds),
        compiler_params=params(),
        cost_estimate=cost(2 * keep_a.size, 16 * keep_a.size),
        name="fold",
    )(place, keep_a, keep_b, came_a, came_b)


def halve_kernel(field, came, part_a, part_b, both):
    vectors = part_a.shape[3]
    for i, piece in enumerate((field, came)):
        for j, part in enumerate((part_a, part_b)):
            value = piece[0, :, :, j * vectors : (j + 1) * vectors]
            part[i] = value
            both[j, i] = value


def pair_kernel(own_a, own_b, came_a, came_b, part_a, part_b, both):
    count = own_a.shape[0]
    for j, (own, came, part) in enumerate(((own_a, came_a, part_a), (own_b, came_b, part_b))):
        part[:count] = own[...]
        part[count:] = came[...]
        both[j] = came[...]


def both_kernel(came_a, came_b, both):
    both[0] = came_a[...]
    both[1] = came_b[...]


def gather(kernel, *pieces):
    count, moms, rows, width = pieces[0].shape
    shapes = {
        halve_kernel: [(2 * count, moms, rows, width // 2)] * 2 + [(2, 2 * count, moms, rows, width // 2)],
        pair_kernel: [(2 * count, moms, rows, width)] * 2 + [(2, count, moms, rows, width)],
        both_kernel: [(2, count, moms, rows, width)],
    }[kernel]
    vmem = pl.BlockSpec(memory_space=pltpu.VMEM)
    return pl.pallas_call(
        kernel,
        out_shape=[jax.ShapeDtypeStruct(shape, BF16) for shape in shapes],
        in_specs=[vmem] * len(pieces),
        out_specs=[vmem] * len(shapes),
        compiler_params=params(),
        cost_estimate=cost(0, 4 * len(pieces) * pieces[0].size),
        name="gather",
    )(*pieces)


def prepare_kernel(groups, place, *refs):
    fields, (left, sink) = refs[:-2], refs[-2:]
    moms, piece_rows, vectors = fields[0].shape[2:]
    columns = left.shape[1] // (2 * moms)
    per = columns // piece_rows
    x = place[X]
    for t in range(2):
        for p, here in enumerate((place[HERE_A], place[HERE_B])):
            j = 0
            for field in fields[t * groups : (t + 1) * groups]:
                for i in range(field.shape[1]):
                    q = here ^ j
                    j += 1
                    to_sink = pl.ds(pl.multiple_of(p * vectors + q * piece_rows, piece_rows), piece_rows)
                    for m in range(moms):
                        sink[t, m, to_sink] = field[p, i, m]

                    @pl.when(q // per == x)
                    def _(field=field, i=i, q=q):
                        for m in range(moms):
                            rows = field[p, i, m]
                            at = pl.multiple_of(2 * m * columns + (q - x * per) * piece_rows, piece_rows)
                            up, down = pl.ds(at, piece_rows), pl.ds(at + columns, piece_rows)
                            if p == 0:
                                left[t, up, :vectors] = rows
                                left[t, down, vectors:] = rows
                            else:
                                left[t, up, vectors:] = rows
                                left[t, down, :vectors] = -rows


def prepare(own, oth, columns, place):
    moms, piece_rows, vectors = own[0].shape[2:]
    vmem = pl.BlockSpec(memory_space=pltpu.VMEM)
    return pl.pallas_call(
        functools.partial(prepare_kernel, len(own)),
        out_shape=(
            jax.ShapeDtypeStruct((2, 2 * moms * columns, 2 * vectors), BF16),
            jax.ShapeDtypeStruct((2, moms, 2 * vectors, vectors), BF16),
        ),
        in_specs=[pl.BlockSpec(memory_space=pltpu.SMEM)] + [vmem] * (len(own) + len(oth)),
        out_specs=(vmem, vmem),
        compiler_params=params(),
        cost_estimate=cost(0, 16 * own[-1].size),
        name="prepare",
    )(place, *own, *oth)


def dress_kernel(count, chained, place, other_src, other_snk, left, sink, *refs):
    mine, near = refs[:count], refs[count : 2 * count]
    out, panel = refs[2 * count + chained :]
    moms, width, vectors = sink.shape[1:]
    columns = out.shape[3]
    pair = pl.program_id(0)
    x, z = place[X], place[Z]
    src, snk = other_src[pair], other_snk[pair]
    block = mine[0].shape[2]
    for k in range(count):
        base = (z ^ k) * vectors
        at_mine = pl.ds(pl.multiple_of(base + x * block, block), block)
        at_near = pl.ds(pl.multiple_of(base + (1 - x) * block, block), block)
        for part in range(2):
            lanes = slice(part * vectors, (part + 1) * vectors)
            panel[at_mine, lanes] = mine[k][0, part]
            panel[at_near, lanes] = near[k][0, part]

    contract = (((1,), (1,)), ((), ()))
    right = lax.dot_general(left[src], panel[...], contract, preferred_element_type=F32).astype(BF16)
    for m in range(moms):
        part = right[2 * m * columns : 2 * (m + 1) * columns]
        rows = jnp.concatenate([part[:, k * vectors : (k + 1) * vectors] for k in range(count)], 0)
        both = lax.dot_general(rows, sink[snk, m], contract, preferred_element_type=F32)
        for k in range(count):
            at = slice(k * vectors, (k + 1) * vectors)
            re = both[2 * k * columns : (2 * k + 1) * columns]
            im = both[(2 * k + 1) * columns : (2 * k + 2) * columns]
            out[0, m, 0, :, at] = (re[:, :vectors] - im[:, vectors:]).astype(BF16)
            out[0, m, 1, :, at] = (re[:, vectors:] + im[:, :vectors]).astype(BF16)


def dress(out, out_shape, first_pair, pairs, mine, near, left, sink, place, other_src, other_snk):
    _, _, block, vectors = mine[0][0].shape
    count = len(mine)
    moms = sink.shape[1]
    columns = out_shape.shape[3]
    whole = pl.BlockSpec(memory_space=pltpu.VMEM)
    chunks = [
        pl.BlockSpec((1, 2, block, vectors), lambda p, *_, first=first: (p + first, 0, 0, 0))
        for _, first in (*mine, *near)
    ]
    chained = out is not None
    operands = [left, sink, *(part for part, _ in (*mine, *near))] + ([out] if chained else [])
    in_specs = [whole, whole] + chunks + [pl.BlockSpec(memory_space=pl.ANY)] * chained
    macs = pairs * count * 2 * (2 * moms * columns) * (2 * vectors) * vectors
    return pl.pallas_call(
        functools.partial(dress_kernel, count, chained),
        out_shape=out_shape,
        grid_spec=pltpu.PrefetchScalarGridSpec(
            num_scalar_prefetch=3,
            grid=(pairs,),
            in_specs=in_specs,
            out_specs=pl.BlockSpec(
                (1, moms, 2, columns, count * vectors), lambda p, *_: (p + first_pair, 0, 0, 0, 0)
            ),
            scratch_shapes=[pltpu.VMEM((count * 2 * block, 2 * vectors), BF16)],
        ),
        input_output_aliases={3 + len(operands) - 1: 0} if chained else {},
        compiler_params=params(1),
        cost_estimate=cost(2 * macs, 2**21),
        name="dress",
    )(place, other_src[first_pair : first_pair + pairs], other_snk[first_pair : first_pair + pairs], *operands)


CHUNKS = (2, 2, 2, 2)
HOOKS = [
    [],
    [("z", 3, 0)],
    [("x", 0, 0)],
    [("x", 0, 1), ("z", 1, 0)],
    [("x", 3, 0)],
    [("z", 3, 1), ("x", 1, 0)],
    [("z", 2, 0), ("x", 3, 1), ("z", 1, 1)],
]
CALLS = ((0, 2), (2, 2))
AFTER = {("x", 2, 1): [("x", 1, 1)]}
FROM = {("z", 2, 1): 4}


def exchange(value, axis, mask, among=lambda i: True):
    return lax.ppermute(value, axis, [(i, i ^ mask) for i in range(lax.axis_size(axis)) if among(i)])


def fast(eigvecs, momenta, pair_list, panels):
    vectors = eigvecs.shape[4]
    pair_count, _, rows, width = panels.shape
    moms = momenta.shape[0]
    space_count = lax.axis_size("space")
    spins = width // vectors
    space = lax.axis_index("space")
    tm = lax.axis_index("tm")
    x, z = space & 1, space >> 1
    low, high = z & 1, z >> 1
    where = [space, x, z, low, high, x * 4 + low * 2 + high, low * 4 + x * 2 + high]
    place = jnp.stack([value.astype(jnp.int32) for value in (*where, *momenta.reshape(-1))])
    other = (pair_list != tm).astype(jnp.int32)
    other_src, other_snk = other[:, 0], other[:, 1]

    factor = 1.0 / math.sqrt(6.0 * eigvecs.shape[3] * space_count * vectors)
    plan = [
        (d, c * (pair_count // n), pair_count // n) for d, n in enumerate(CHUNKS) for c in range(n)
    ]
    send_a, send_b, keep_a, keep_b = gram_halves(eigvecs[0], moms, place, factor)
    blocks = cut_panels(panels, vectors, plan, CUT_VMEM, place)

    raw, held, steps = {}, {}, []

    def fetch(name):
        if name not in raw:
            hop, d, c = name
            value = blocks[d, c] if hop == "z" or d == 0 else fetch(("z", d, c))
            if name in FROM:
                value, _ = lax.optimization_barrier((value, steps[FROM[name]]))
            raw[name] = exchange(meet(value, AFTER.get(name)), "space", 2 * d if hop == "z" else 1)
        held.setdefault(name, raw[name])
        return raw[name]

    def meet(value, names):
        if not names:
            return value
        for name in names:
            fetch(name)
        value, *came = lax.optimization_barrier((value, *(held[name] for name in names)))
        held.update(zip(names, came))
        return value

    along_x, low_z, high_z = 1, 2, 4

    def step(*sends):
        came = [exchange(value, "space", mask) for value, mask in sends]
        came[0] = meet(came[0], HOOKS[len(steps)])
        steps.append(came[0])
        return came

    came = step((send_a, along_x), (send_b, low_z))
    send_a, send_b, keep_a, keep_b = fold(fold_kernel, keep_a, keep_b, *came, place)
    came = step((send_a, low_z), (send_b, along_x))
    send, keep = fold(join_kernel, keep_a, keep_b, *came, place)
    (came,) = step((send, high_z))
    field = (keep + came.astype(F32)).astype(BF16)[None]
    (came,) = step((field, high_z))
    own, oth = [], []

    def share(both):
        own.append(both)
        oth.append(exchange(both, "tm", 1))

    *parts, both = gather(halve_kernel, field, came)
    share(both)
    came = step((parts[0], low_z), (parts[1], along_x))
    *parts, both = gather(pair_kernel, *parts, *came)
    share(both)
    came = step((parts[0], along_x), (parts[1], low_z))
    share(*gather(both_kernel, *came))
    oth[2] = meet(oth[2], HOOKS[6])

    columns = width // space_count
    out_shape = jax.ShapeDtypeStruct((pair_count, moms, 2, columns, width), BF16)

    def part(hop, d, first):
        c, at = divmod(first, pair_count // CHUNKS[d])
        if (hop, d) == ("z", 0):
            return blocks[0, c], at
        fetch((hop, d, c))
        return held[hop, d, c], at

    left, sink = prepare(own, oth, columns, place)
    out = None
    dists = range(spins)
    for first, pairs in CALLS:
        mine = [part("z", d, first) for d in dists]
        near = [part("x", d, first) for d in dists]
        out = dress(
            out, out_shape, first, pairs, mine, near, left, sink, place, other_src, other_snk
        )
    return out


def phased_block(cosine, sine_part, real_part, imag_part):
    cos_col = cosine[:, None]
    sin_col = sine_part[:, None]
    wave_re = cos_col * real_part + sin_col * imag_part
    wave_im = cos_col * imag_part - sin_col * real_part
    upper = jnp.concatenate([wave_re, wave_im], -1)
    lower = jnp.concatenate([wave_im, -wave_re], -1)
    return jnp.stack([upper, lower], -4).astype(jnp.bfloat16)


def general(eigvecs, momenta, pair_list, panels):
    slice_count, _, colors, slab_sites, vectors = eigvecs.shape
    mom_count = momenta.shape[0]
    space_count = lax.axis_size("space")
    first_site = lax.axis_index("space") * slab_sites
    site_index = first_site + jnp.arange(slab_sites, dtype=jnp.int32)
    xpos = site_index % LX
    ypos = site_index // LX % LX
    zpos = site_index // (LX * LX)
    wave = (
        momenta[:, 0:1] * xpos[None, :]
        + momenta[:, 1:2] * ypos[None, :]
        + momenta[:, 2:3] * zpos[None, :]
    )
    wave = jnp.mod(wave, LX)
    angle = wave.astype(jnp.float32) * jnp.float32(2.0 * math.pi / LX)
    cosine = jnp.cos(angle)
    sine_part = jnp.sin(angle)
    factor = 1.0 / math.sqrt(6.0 * slab_sites * space_count * vectors)
    real_part = eigvecs[:, 0].astype(jnp.float32)
    imag_part = eigvecs[:, 1].astype(jnp.float32)
    phased_all = jnp.concatenate(
        [
            phased_block(cosine[moment], sine_part[moment], real_part, imag_part)
            for moment in range(mom_count)
        ],
        -1,
    )
    phased_all = phased_all.reshape(slice_count, 2, colors, slab_sites, mom_count, 2 * vectors)
    gram_local = jnp.einsum(
        "trcsk,trcsml->tmkl", eigvecs, phased_all, preferred_element_type=jnp.float32
    )
    gram_local = factor * gram_local
    summed = lax.psum(gram_local, "space")
    own_fields = summed.astype(jnp.bfloat16)
    meson_fields = lax.all_gather(own_fields, "tm", axis=0, tiled=True)
    pair_count = pair_list.shape[0]
    panel_rows = panels.shape[2]
    panel_width = panels.shape[3]
    spins = panel_width // vectors
    source_fields = jnp.take(meson_fields, pair_list[:, 0], axis=0).reshape(
        pair_count, mom_count, vectors, 2, vectors
    )
    sink_fields = jnp.take(meson_fields, pair_list[:, 1], axis=0).reshape(
        pair_count, mom_count, vectors, 2, vectors
    )
    panel_parts = panels.reshape(pair_count, 2, panel_rows, spins, vectors)
    panel_re = panel_parts[:, 0]
    panel_im = panel_parts[:, 1]
    panel_mix = jnp.stack(
        [jnp.stack([panel_re, panel_im], 1), jnp.stack([panel_im, -panel_re], 1)], 1
    )
    right_dressed = jnp.einsum(
        "porxbk,pmlrk->pmoxbl", panel_mix, source_fields, preferred_element_type=jnp.float32
    )
    right_dressed = right_dressed.astype(jnp.bfloat16).reshape(
        pair_count * mom_count, 2, panel_rows, panel_width
    )
    turned = lax.all_to_all(right_dressed, "space", split_axis=3, concat_axis=2, tiled=True)
    column_count = turned.shape[3]
    turned = turned.reshape(pair_count, mom_count, 2, spins, vectors, column_count)
    turned_re = turned[:, :, 0]
    turned_im = turned[:, :, 1]
    mixed_parts = jnp.stack(
        [jnp.stack([turned_re, -turned_im], 2), jnp.stack([turned_im, turned_re], 2)], 2
    )
    dressed = jnp.einsum(
        "pmorajc,pmkrj->pmocak", mixed_parts, sink_fields, preferred_element_type=jnp.float32
    )
    return dressed.reshape(pair_count, mom_count, 2, column_count, panel_width).astype(jnp.bfloat16)


def local(eigvecs, momenta, pair_list, panels):
    slices, _, _, sites, vectors = eigvecs.shape
    pairs, _, rows, width = panels.shape
    space_count = lax.axis_size("space")
    spins = width // vectors
    fits = (
        slices == 1
        and lax.axis_size("tm") == 2
        and space_count == 2 * spins
        and spins == 4
        and rows * space_count == width
        and rows % 128 == 0
        and (vectors // space_count) % 16 == 0
        and sites % 16 == 0
        and pairs % 2 == 0
        and momenta.shape[0] <= 8
    )
    return (fast if fits else general)(eigvecs, momenta, pair_list, panels)


def solution(mesh):
    placed = (
        P(("cfg", "tm"), None, None, "space", None),
        P(),
        P("tm", None),
        P(("cfg", "tm"), None, "space", None),
    )
    return jax.shard_map(
        local,
        mesh=mesh,
        in_specs=placed,
        out_specs=P(("cfg", "tm"), None, None, "space", None),
        check_vma=False,
    )
```

```python
import functools
import math

import jax
import jax.numpy as jnp
from jax import lax
from jax.experimental import pallas as pl
from jax.experimental.pallas import tpu as pltpu
from jax.sharding import PartitionSpec as P

LX = 64
LX_BITS = LX.bit_length() - 1
F32, BF16 = jnp.float32, jnp.bfloat16
SPACE, X, Z, Z_LOW, Z_HIGH, HERE_A, HERE_B, MOMENTA = range(8)
VMEM_LIMIT = 24 * 1024 * 1024
CUT_VMEM = 24 * 1024 * 1024


def params(steps=0):
    return pltpu.CompilerParams(
        vmem_limit_bytes=VMEM_LIMIT, dimension_semantics=("arbitrary",) * steps or None
    )


def cost(flops, bytes_accessed):
    return pl.CostEstimate(flops=int(flops), bytes_accessed=int(bytes_accessed), transcendentals=0)


def gram_kernel(factor, place, eig, send_a, send_b, keep_a, keep_b, phased, total):
    colors, sites, vectors = eig.shape[1:]
    moms, half = send_a.shape[:2]
    site = place[SPACE] * sites + lax.broadcasted_iota(jnp.int32, (sites, 128), 0)
    lane = lax.broadcasted_iota(jnp.int32, (sites, 128), 1)
    coords = (site & (LX - 1), (site >> LX_BITS) & (LX - 1), site >> (2 * LX_BITS))
    wave = jnp.zeros((sites, 128), jnp.int32)
    for m in range(moms):
        mine = sum(place[MOMENTA + 3 * m + j] * coords[j] for j in range(3))
        wave = jnp.where(lane == m, mine, wave)
    angle = (wave & (LX - 1)).astype(F32) * F32(2.0 * math.pi / LX)
    cosine, sine = jnp.cos(angle), jnp.sin(angle)
    rows = colors * sites
    both = eig[...].reshape(2 * rows, vectors)
    for m in range(moms):
        c, s = cosine[:, m : m + 1], sine[:, m : m + 1]
        for color in range(colors):
            re, im = eig[0, color].astype(F32), eig[1, color].astype(F32)
            wave_re, wave_im = c * re + s * im, c * im - s * re
            at = color * sites
            phased[at : at + sites, :vectors] = wave_re.astype(BF16)
            phased[at : at + sites, vectors:] = wave_im.astype(BF16)
            at += rows
            phased[at : at + sites, :vectors] = wave_im.astype(BF16)
            phased[at : at + sites, vectors:] = (-wave_re).astype(BF16)
        total[...] = factor * lax.dot_general(
            both, phased[...], (((0,), (0,)), ((), ())), preferred_element_type=F32
        )
        for send, keep, bit, lanes in (
            (send_a, keep_a, place[X], slice(None, vectors)),
            (send_b, keep_b, place[Z_LOW], slice(vectors, None)),
        ):
            send[m] = total[pl.ds(pl.multiple_of((1 - bit) * half, half), half), lanes].astype(BF16)
            keep[m] = total[pl.ds(pl.multiple_of(bit * half, half), half), lanes]


def gram_halves(eig, moms, place, factor):
    _, colors, sites, vectors = eig.shape
    shape = (moms, vectors // 2, vectors)
    smem = pl.BlockSpec(memory_space=pltpu.SMEM)
    vmem = pl.BlockSpec(memory_space=pltpu.VMEM)
    return pl.pallas_call(
        functools.partial(gram_kernel, factor),
        out_shape=[jax.ShapeDtypeStruct(shape, kind) for kind in (BF16, BF16, F32, F32)],
        in_specs=[smem, vmem],
        out_specs=[vmem] * 4,
        scratch_shapes=[
            pltpu.VMEM((2 * colors * sites, 2 * vectors), BF16),
            pltpu.VMEM((vectors, 2 * vectors), F32),
        ],
        compiler_params=params(),
        cost_estimate=cost(4 * colors * sites * vectors * moms * 2 * vectors, 3 * 2**20),
        name="gram",
    )(place, eig)


def cut_kernel(plan, place, panels, *refs):
    cuts, sems = refs[:-1], refs[-1]
    vectors = cuts[0].shape[3]
    copies = []
    for i, (d, first, _) in enumerate(plan):
        lanes = pl.ds(pl.multiple_of((place[Z] ^ d) * vectors, vectors), vectors)
        source = panels.at[first : first + cuts[i].shape[0], :, :, lanes]
        copies.append(pltpu.make_async_copy(source, cuts[i], sems.at[i]))
        copies[-1].start()
    for copy in copies:
        copy.wait()


def cut_panels(panels, vectors, plan, vmem, place):
    cuts = pl.pallas_call(
        functools.partial(cut_kernel, plan),
        out_shape=[jax.ShapeDtypeStruct((size, *panels.shape[1:3], vectors), BF16) for _, _, size in plan],
        in_specs=[pl.BlockSpec(memory_space=pltpu.SMEM), pl.BlockSpec(memory_space=pl.ANY)],
        out_specs=[pl.BlockSpec(memory_space=pltpu.VMEM)] * len(plan),
        scratch_shapes=[pltpu.SemaphoreType.DMA((len(plan),))],
        compiler_params=pltpu.CompilerParams(vmem_limit_bytes=vmem),
        cost_estimate=cost(0, 4 * panels.size),
        name="cut",
    )(place, panels)
    return {(d, first // size): cut for (d, first, size), cut in zip(plan, cuts)}


def fold_kernel(place, keep_a, keep_b, came_a, came_b, send_a, send_b, left_a, left_b):
    half = send_a.shape[1]
    for keep, came, bit, send, left in (
        (keep_a, came_a, place[Z_LOW], send_a, left_a),
        (keep_b, came_b, place[X], send_b, left_b),
    ):
        own = pl.ds(pl.multiple_of(bit * half, half), half)
        off = pl.ds(pl.multiple_of((1 - bit) * half, half), half)
        left[...] = keep[:, own, :] + came[:, own, :].astype(F32)
        send[...] = (keep[:, off, :] + came[:, off, :].astype(F32)).astype(BF16)


def join_kernel(place, keep_a, keep_b, came_a, came_b, send, left):
    half, width = send.shape[1:]
    bit = place[Z_HIGH]
    own = pl.ds(pl.multiple_of(bit * half, half), half)
    off = pl.ds(pl.multiple_of((1 - bit) * half, half), half)
    for keep, came, lanes in (
        (keep_a, came_a, slice(None, width // 2)),
        (keep_b, came_b, slice(width // 2, None)),
    ):
        left[:, :, lanes] = keep[:, own, :] + came[:, own, :].astype(F32)
        send[:, :, lanes] = (keep[:, off, :] + came[:, off, :].astype(F32)).astype(BF16)


def fold(kernel, keep_a, keep_b, came_a, came_b, place):
    moms, rows, width = keep_a.shape
    if kernel is join_kernel:
        shape, kinds = (moms, rows // 2, 2 * width), (BF16, F32)
    else:
        shape, kinds = (moms, rows // 2, width), (BF16, BF16, F32, F32)
    vmem = pl.BlockSpec(memory_space=pltpu.VMEM)
    return pl.pallas_call(
        kernel,
        out_shape=[jax.ShapeDtypeStruct(shape, kind) for kind in kinds],
        in_specs=[pl.BlockSpec(memory_space=pltpu.SMEM)] + [vmem] * 4,
        out_specs=[vmem] * len(kinds),
        compiler_params=params(),
        cost_estimate=cost(2 * keep_a.size, 16 * keep_a.size),
        name="fold",
    )(place, keep_a, keep_b, came_a, came_b)


def halve_kernel(field, came, part_a, part_b, both):
    vectors = part_a.shape[3]
    for i, piece in enumerate((field, came)):
        for j, part in enumerate((part_a, part_b)):
            value = piece[0, :, :, j * vectors : (j + 1) * vectors]
            part[i] = value
            both[j, i] = value


def pair_kernel(own_a, own_b, came_a, came_b, part_a, part_b, both):
    count = own_a.shape[0]
    for j, (own, came, part) in enumerate(((own_a, came_a, part_a), (own_b, came_b, part_b))):
        part[:count] = own[...]
        part[count:] = came[...]
        both[j] = came[...]


def both_kernel(came_a, came_b, both):
    both[0] = came_a[...]
    both[1] = came_b[...]


def gather(kernel, *pieces):
    count, moms, rows, width = pieces[0].shape
    shapes = {
        halve_kernel: [(2 * count, moms, rows, width // 2)] * 2 + [(2, 2 * count, moms, rows, width // 2)],
        pair_kernel: [(2 * count, moms, rows, width)] * 2 + [(2, count, moms, rows, width)],
        both_kernel: [(2, count, moms, rows, width)],
    }[kernel]
    vmem = pl.BlockSpec(memory_space=pltpu.VMEM)
    return pl.pallas_call(
        kernel,
        out_shape=[jax.ShapeDtypeStruct(shape, BF16) for shape in shapes],
        in_specs=[vmem] * len(pieces),
        out_specs=[vmem] * len(shapes),
        compiler_params=params(),
        cost_estimate=cost(0, 4 * len(pieces) * pieces[0].size),
        name="gather",
    )(*pieces)


def prepare_kernel(groups, place, *refs):
    fields, (left, sink) = refs[:-2], refs[-2:]
    moms, piece_rows, vectors = fields[0].shape[2:]
    columns = left.shape[1] // (2 * moms)
    per = columns // piece_rows
    x = place[X]
    for t in range(2):
        for p, here in enumerate((place[HERE_A], place[HERE_B])):
            j = 0
            for field in fields[t * groups : (t + 1) * groups]:
                for i in range(field.shape[1]):
                    q = here ^ j
                    j += 1
                    to_sink = pl.ds(pl.multiple_of(p * vectors + q * piece_rows, piece_rows), piece_rows)
                    for m in range(moms):
                        sink[t, m, to_sink] = field[p, i, m]

                    @pl.when(q // per == x)
                    def _(field=field, i=i, q=q):
                        for m in range(moms):
                            rows = field[p, i, m]
                            at = pl.multiple_of(2 * m * columns + (q - x * per) * piece_rows, piece_rows)
                            up, down = pl.ds(at, piece_rows), pl.ds(at + columns, piece_rows)
                            if p == 0:
                                left[t, up, :vectors] = rows
                                left[t, down, vectors:] = rows
                            else:
                                left[t, up, vectors:] = rows
                                left[t, down, :vectors] = -rows


def prepare(own, oth, columns, place):
    moms, piece_rows, vectors = own[0].shape[2:]
    vmem = pl.BlockSpec(memory_space=pltpu.VMEM)
    return pl.pallas_call(
        functools.partial(prepare_kernel, len(own)),
        out_shape=(
            jax.ShapeDtypeStruct((2, 2 * moms * columns, 2 * vectors), BF16),
            jax.ShapeDtypeStruct((2, moms, 2 * vectors, vectors), BF16),
        ),
        in_specs=[pl.BlockSpec(memory_space=pltpu.SMEM)] + [vmem] * (len(own) + len(oth)),
        out_specs=(vmem, vmem),
        compiler_params=params(),
        cost_estimate=cost(0, 16 * own[-1].size),
        name="prepare",
    )(place, *own, *oth)


def dress_kernel(count, chained, place, other_src, other_snk, left, sink, *refs):
    mine, near = refs[:count], refs[count : 2 * count]
    out, panel = refs[2 * count + chained :]
    moms, width, vectors = sink.shape[1:]
    columns = out.shape[3]
    pair = pl.program_id(0)
    x, z = place[X], place[Z]
    src, snk = other_src[pair], other_snk[pair]
    block = mine[0].shape[2]
    for k in range(count):
        base = (z ^ k) * vectors
        at_mine = pl.ds(pl.multiple_of(base + x * block, block), block)
        at_near = pl.ds(pl.multiple_of(base + (1 - x) * block, block), block)
        for part in range(2):
            lanes = slice(part * vectors, (part + 1) * vectors)
            panel[at_mine, lanes] = mine[k][0, part]
            panel[at_near, lanes] = near[k][0, part]

    contract = (((1,), (1,)), ((), ()))
    right = lax.dot_general(left[src], panel[...], contract, preferred_element_type=F32).astype(BF16)
    for m in range(moms):
        part = right[2 * m * columns : 2 * (m + 1) * columns]
        rows = jnp.concatenate([part[:, k * vectors : (k + 1) * vectors] for k in range(count)], 0)
        both = lax.dot_general(rows, sink[snk, m], contract, preferred_element_type=F32)
        for k in range(count):
            at = slice(k * vectors, (k + 1) * vectors)
            re = both[2 * k * columns : (2 * k + 1) * columns]
            im = both[(2 * k + 1) * columns : (2 * k + 2) * columns]
            out[0, m, 0, :, at] = (re[:, :vectors] - im[:, vectors:]).astype(BF16)
            out[0, m, 1, :, at] = (re[:, vectors:] + im[:, :vectors]).astype(BF16)


def dress(out, out_shape, first_pair, pairs, mine, near, left, sink, place, other_src, other_snk):
    _, _, block, vectors = mine[0][0].shape
    count = len(mine)
    moms = sink.shape[1]
    columns = out_shape.shape[3]
    whole = pl.BlockSpec(memory_space=pltpu.VMEM)
    chunks = [
        pl.BlockSpec((1, 2, block, vectors), lambda p, *_, first=first: (p + first, 0, 0, 0))
        for _, first in (*mine, *near)
    ]
    chained = out is not None
    operands = [left, sink, *(part for part, _ in (*mine, *near))] + ([out] if chained else [])
    in_specs = [whole, whole] + chunks + [pl.BlockSpec(memory_space=pl.ANY)] * chained
    macs = pairs * count * 2 * (2 * moms * columns) * (2 * vectors) * vectors
    return pl.pallas_call(
        functools.partial(dress_kernel, count, chained),
        out_shape=out_shape,
        grid_spec=pltpu.PrefetchScalarGridSpec(
            num_scalar_prefetch=3,
            grid=(pairs,),
            in_specs=in_specs,
            out_specs=pl.BlockSpec(
                (1, moms, 2, columns, count * vectors), lambda p, *_: (p + first_pair, 0, 0, 0, 0)
            ),
            scratch_shapes=[pltpu.VMEM((count * 2 * block, 2 * vectors), BF16)],
        ),
        input_output_aliases={3 + len(operands) - 1: 0} if chained else {},
        compiler_params=params(1),
        cost_estimate=cost(2 * macs, 2**21),
        name="dress",
    )(place, other_src[first_pair : first_pair + pairs], other_snk[first_pair : first_pair + pairs], *operands)


CHUNKS = (2, 2, 2, 2)
HOOKS = [
    [],
    [("z", 3, 0)],
    [("x", 0, 0)],
    [("x", 0, 1), ("z", 1, 0)],
    [("x", 3, 0)],
    [("z", 3, 1), ("x", 1, 0), ("z", 1, 1)],
    [("z", 2, 0), ("x", 3, 1)],
]
CALLS = ((0, 2), (2, 2))
AFTER = {("x", 2, 1): [("x", 1, 1)]}
FROM = {("z", 2, 1): 4}


def exchange(value, axis, mask, among=lambda i: True):
    return lax.ppermute(value, axis, [(i, i ^ mask) for i in range(lax.axis_size(axis)) if among(i)])


def fast(eigvecs, momenta, pair_list, panels):
    vectors = eigvecs.shape[4]
    pair_count, _, rows, width = panels.shape
    moms = momenta.shape[0]
    space_count = lax.axis_size("space")
    spins = width // vectors
    space = lax.axis_index("space")
    tm = lax.axis_index("tm")
    x, z = space & 1, space >> 1
    low, high = z & 1, z >> 1
    where = [space, x, z, low, high, x * 4 + low * 2 + high, low * 4 + x * 2 + high]
    place = jnp.stack([value.astype(jnp.int32) for value in (*where, *momenta.reshape(-1))])
    other = (pair_list != tm).astype(jnp.int32)
    other_src, other_snk = other[:, 0], other[:, 1]

    factor = 1.0 / math.sqrt(6.0 * eigvecs.shape[3] * space_count * vectors)
    plan = [
        (d, c * (pair_count // n), pair_count // n) for d, n in enumerate(CHUNKS) for c in range(n)
    ]
    send_a, send_b, keep_a, keep_b = gram_halves(eigvecs[0], moms, place, factor)
    blocks = cut_panels(panels, vectors, plan, CUT_VMEM, place)

    raw, held, steps = {}, {}, []

    def fetch(name):
        if name not in raw:
            hop, d, c = name
            value = blocks[d, c] if hop == "z" or d == 0 else fetch(("z", d, c))
            if name in FROM:
                value, _ = lax.optimization_barrier((value, steps[FROM[name]]))
            raw[name] = exchange(meet(value, AFTER.get(name)), "space", 2 * d if hop == "z" else 1)
        held.setdefault(name, raw[name])
        return raw[name]

    def meet(value, names):
        if not names:
            return value
        for name in names:
            fetch(name)
        value, *came = lax.optimization_barrier((value, *(held[name] for name in names)))
        held.update(zip(names, came))
        return value

    along_x, low_z, high_z = 1, 2, 4

    def step(*sends):
        came = [exchange(value, "space", mask) for value, mask in sends]
        came[0] = meet(came[0], HOOKS[len(steps)])
        steps.append(came[0])
        return came

    came = step((send_a, along_x), (send_b, low_z))
    send_a, send_b, keep_a, keep_b = fold(fold_kernel, keep_a, keep_b, *came, place)
    came = step((send_a, low_z), (send_b, along_x))
    send, keep = fold(join_kernel, keep_a, keep_b, *came, place)
    (came,) = step((send, high_z))
    field = (keep + came.astype(F32)).astype(BF16)[None]
    (came,) = step((field, high_z))
    own, oth = [], []

    def share(both):
        own.append(both)
        oth.append(exchange(both, "tm", 1))

    *parts, both = gather(halve_kernel, field, came)
    share(both)
    came = step((parts[0], low_z), (parts[1], along_x))
    *parts, both = gather(pair_kernel, *parts, *came)
    share(both)
    came = step((parts[0], along_x), (parts[1], low_z))
    share(*gather(both_kernel, *came))
    oth[2] = meet(oth[2], HOOKS[6])

    columns = width // space_count
    out_shape = jax.ShapeDtypeStruct((pair_count, moms, 2, columns, width), BF16)

    def part(hop, d, first):
        c, at = divmod(first, pair_count // CHUNKS[d])
        if (hop, d) == ("z", 0):
            return blocks[0, c], at
        fetch((hop, d, c))
        return held[hop, d, c], at

    left, sink = prepare(own, oth, columns, place)
    out = None
    dists = range(spins)
    for first, pairs in CALLS:
        mine = [part("z", d, first) for d in dists]
        near = [part("x", d, first) for d in dists]
        out = dress(
            out, out_shape, first, pairs, mine, near, left, sink, place, other_src, other_snk
        )
    return out


def phased_block(cosine, sine_part, real_part, imag_part):
    cos_col = cosine[:, None]
    sin_col = sine_part[:, None]
    wave_re = cos_col * real_part + sin_col * imag_part
    wave_im = cos_col * imag_part - sin_col * real_part
    upper = jnp.concatenate([wave_re, wave_im], -1)
    lower = jnp.concatenate([wave_im, -wave_re], -1)
    return jnp.stack([upper, lower], -4).astype(jnp.bfloat16)


def general(eigvecs, momenta, pair_list, panels):
    slice_count, _, colors, slab_sites, vectors = eigvecs.shape
    mom_count = momenta.shape[0]
    space_count = lax.axis_size("space")
    first_site = lax.axis_index("space") * slab_sites
    site_index = first_site + jnp.arange(slab_sites, dtype=jnp.int32)
    xpos = site_index % LX
    ypos = site_index // LX % LX
    zpos = site_index // (LX * LX)
    wave = (
        momenta[:, 0:1] * xpos[None, :]
        + momenta[:, 1:2] * ypos[None, :]
        + momenta[:, 2:3] * zpos[None, :]
    )
    wave = jnp.mod(wave, LX)
    angle = wave.astype(jnp.float32) * jnp.float32(2.0 * math.pi / LX)
    cosine = jnp.cos(angle)
    sine_part = jnp.sin(angle)
    factor = 1.0 / math.sqrt(6.0 * slab_sites * space_count * vectors)
    real_part = eigvecs[:, 0].astype(jnp.float32)
    imag_part = eigvecs[:, 1].astype(jnp.float32)
    phased_all = jnp.concatenate(
        [
            phased_block(cosine[moment], sine_part[moment], real_part, imag_part)
            for moment in range(mom_count)
        ],
        -1,
    )
    phased_all = phased_all.reshape(slice_count, 2, colors, slab_sites, mom_count, 2 * vectors)
    gram_local = jnp.einsum(
        "trcsk,trcsml->tmkl", eigvecs, phased_all, preferred_element_type=jnp.float32
    )
    gram_local = factor * gram_local
    summed = lax.psum(gram_local, "space")
    own_fields = summed.astype(jnp.bfloat16)
    meson_fields = lax.all_gather(own_fields, "tm", axis=0, tiled=True)
    pair_count = pair_list.shape[0]
    panel_rows = panels.shape[2]
    panel_width = panels.shape[3]
    spins = panel_width // vectors
    source_fields = jnp.take(meson_fields, pair_list[:, 0], axis=0).reshape(
        pair_count, mom_count, vectors, 2, vectors
    )
    sink_fields = jnp.take(meson_fields, pair_list[:, 1], axis=0).reshape(
        pair_count, mom_count, vectors, 2, vectors
    )
    panel_parts = panels.reshape(pair_count, 2, panel_rows, spins, vectors)
    panel_re = panel_parts[:, 0]
    panel_im = panel_parts[:, 1]
    panel_mix = jnp.stack(
        [jnp.stack([panel_re, panel_im], 1), jnp.stack([panel_im, -panel_re], 1)], 1
    )
    right_dressed = jnp.einsum(
        "porxbk,pmlrk->pmoxbl", panel_mix, source_fields, preferred_element_type=jnp.float32
    )
    right_dressed = right_dressed.astype(jnp.bfloat16).reshape(
        pair_count * mom_count, 2, panel_rows, panel_width
    )
    turned = lax.all_to_all(right_dressed, "space", split_axis=3, concat_axis=2, tiled=True)
    column_count = turned.shape[3]
    turned = turned.reshape(pair_count, mom_count, 2, spins, vectors, column_count)
    turned_re = turned[:, :, 0]
    turned_im = turned[:, :, 1]
    mixed_parts = jnp.stack(
        [jnp.stack([turned_re, -turned_im], 2), jnp.stack([turned_im, turned_re], 2)], 2
    )
    dressed = jnp.einsum(
        "pmorajc,pmkrj->pmocak", mixed_parts, sink_fields, preferred_element_type=jnp.float32
    )
    return dressed.reshape(pair_count, mom_count, 2, column_count, panel_width).astype(jnp.bfloat16)


def local(eigvecs, momenta, pair_list, panels):
    slices, _, _, sites, vectors = eigvecs.shape
    pairs, _, rows, width = panels.shape
    space_count = lax.axis_size("space")
    spins = width // vectors
    fits = (
        slices == 1
        and lax.axis_size("tm") == 2
        and space_count == 2 * spins
        and spins == 4
        and rows * space_count == width
        and rows % 128 == 0
        and (vectors // space_count) % 16 == 0
        and sites % 16 == 0
        and pairs % 2 == 0
        and momenta.shape[0] <= 8
    )
    return (fast if fits else general)(eigvecs, momenta, pair_list, panels)


def solution(mesh):
    placed = (
        P(("cfg", "tm"), None, None, "space", None),
        P(),
        P("tm", None),
        P(("cfg", "tm"), None, "space", None),
    )
    return jax.shard_map(
        local,
        mesh=mesh,
        in_specs=placed,
        out_specs=P(("cfg", "tm"), None, None, "space", None),
        check_vma=False,
    )
```
